32 devices in a mesh: gy: 8 (over z, x), gz: 4 (over y, core).
Axes of the slice: x: 2, y: 2, z: 4, core: 2. Of those that a mesh axis runs over, the one named last changes fastest.
Arguments:
- heat_scalar_window: float32 [128, 32, 2048], P('gy', 'gz'), may hold values from -6 to 6
- flow_speed_vector: bfloat16 [3, 128, 32, 2048], P(None, 'gy', 'gz'), may hold values from -4 to 4
Outputs:
- updated: float32 [128, 32, 2048], P('gy', 'gz')
The draws below stay inside these ranges and needn't reach their ends.
All inputs are finite; a program needn't handle non-finite values.
Results may differ from the reference program's by a relative error of at most 0.0003.
Values sent between devices are 32-bit elements; how exact they have to be, the bound alone decides.
A program may use at most 64 MiB of HBM per device.

```python
import jax
import jax.numpy as jnp
from jax import lax

GRID_SPAN_EAST = 2048
RX = 1
RY = 768
RZ = 192
GRID_SPAN_NORTH = 128
GRID_SPAN_VERTICAL = 32


def block_levels(key, shape, split, smallest, high):
    factor_of = 1.0
    for position, parts in split:
        draws = jax.random.uniform(jax.random.fold_in(jax.random.fold_in(key, 6), position), (parts,), jnp.float32, smallest / len(split), high / len(split))
        factor_of = factor_of * jnp.repeat(jnp.exp(draws), shape[position] // parts).reshape((-1,) + (1,) * (len(shape) - 1 - position))
    return factor_of


def noise(own_key, extent, scale, reach, split=(), kind=jnp.bfloat16):
    entries = jax.random.normal(own_key, extent, jnp.float32) * scale
    if len(split) > 0:
        entries = block_levels(own_key, extent, split, -0.22, 0.18) * entries
    return jnp.clip(entries, min=-reach, max=reach).astype(kind)


def setup_inputs(seed: int = 0) -> dict:
    key_of = jax.random.split(jax.random.key(seed), 3)
    return {
        "heat_scalar_window": noise(key_of[0], (GRID_SPAN_NORTH, GRID_SPAN_VERTICAL, GRID_SPAN_EAST), 1.0, 6.0, ((0, 8), (1, 4)), jnp.float32),
        "flow_speed_vector": noise(key_of[1], (3, GRID_SPAN_NORTH, GRID_SPAN_VERTICAL, GRID_SPAN_EAST), 1.0, 4.0, ((1, 8), (2, 4))),
    }


EXACT = lax.Precision.HIGHEST
thermal_conduction_coefficient = 0.15

def line_inverse(line_count, ratio_value):
    coupling = jnp.float32(ratio_value)
    half_step = 0.5 / coupling
    decay_base = 1.0 + half_step - jnp.sqrt(half_step * (2.0 + half_step))
    places = jnp.arange(line_count, dtype=jnp.float32)
    small_index = jnp.minimum(places[:, None], places[None, :])
    large_index = jnp.maximum(places[:, None], places[None, :])
    span_value = jnp.float32(line_count)
    numer = decay_base ** (large_index - small_index + 1.0) * (1.0 - decay_base ** (2.0 * (small_index + 1.0))) * (1.0 - decay_base ** (2.0 * (span_value - large_index)))
    denom = coupling * (1.0 - decay_base * decay_base) * (1.0 - decay_base ** (2.0 * span_value + 2.0))
    return numer / denom

def known_contribution(heat_scalar_window, flow_speed_vector):
    haloed_array = jnp.pad(heat_scalar_window, 1)
    northern_adjacent = haloed_array[2:, 1:-1, 1:-1]
    southern_adjacent = haloed_array[:-2, 1:-1, 1:-1]
    ceiling_adjacent = haloed_array[1:-1, 2:, 1:-1]
    bottom_adjacent = haloed_array[1:-1, :-2, 1:-1]
    eastern_adjacent = haloed_array[1:-1, 1:-1, 2:]
    western_adjacent = haloed_array[1:-1, 1:-1, :-2]
    laplacian_contribution = eastern_adjacent + western_adjacent + northern_adjacent + southern_adjacent + ceiling_adjacent + bottom_adjacent - 6.0 * heat_scalar_window
    retained_remainder = flow_speed_vector[0].astype(jnp.float32) * (eastern_adjacent - western_adjacent) + flow_speed_vector[1].astype(jnp.float32) * (northern_adjacent - southern_adjacent) + flow_speed_vector[2].astype(jnp.float32) * (ceiling_adjacent - bottom_adjacent)
    return heat_scalar_window + thermal_conduction_coefficient * laplacian_contribution - 0.5 * retained_remainder

def reference(heat_scalar_window, flow_speed_vector):
    forcing_contribution = known_contribution(heat_scalar_window, flow_speed_vector)
    inverse_x = line_inverse(GRID_SPAN_EAST, RX)
    inverse_y = line_inverse(GRID_SPAN_NORTH, RY)
    inverse_z = line_inverse(GRID_SPAN_VERTICAL, RZ)
    along_x = jnp.dot(forcing_contribution, inverse_x, precision=EXACT)
    along_y = jnp.einsum('ab,bzx->azx', inverse_y, along_x, precision=EXACT)
    return jnp.einsum('ab,ybx->yax', inverse_z, along_y, precision=EXACT)
```

```python
import functools

import jax
import jax.numpy as jnp
import numpy as np
from jax import lax
from jax.experimental import pallas as pl
from jax.experimental.pallas import tpu as pltpu
from jax.sharding import PartitionSpec as P

RX = 1
RY = 768
RZ = 192
KAPPA = 0.15
XB = 256
LANES = 128
MESH = pl.DeviceIdType.MESH


def decay(ratio):
    h = 0.5 / ratio
    return 1.0 + h - np.sqrt(h * (2.0 + h))


def line_parts(n, ratio):
    q = decay(ratio)
    i = np.arange(n, dtype=np.float64)
    half = n / 2.0
    rise = q ** (-i + half) * (1.0 - q ** (2.0 * (i + 1.0)))
    fall = q ** (i + 1.0 - half) * (1.0 - q ** (2.0 * (n - i)))
    fall = fall / (ratio * (1.0 - q * q) * (1.0 - q ** (2.0 * n + 2.0)))
    return rise, fall


def line_block(rise, fall):
    n = len(rise)
    small = np.minimum(np.arange(n)[:, None], np.arange(n)[None, :])
    large = np.maximum(np.arange(n)[:, None], np.arange(n)[None, :])
    return rise[small] * fall[large]


def sizes(ny, nz, ly, lz):
    rows = ly * lz
    far_y = rows
    far_z = far_y + 2 * lz
    corner = far_z + nz * ly
    total = corner + -(-2 * nz // 8) * 8
    return rows, far_y, far_z, corner, total


def tables(ny, nz, ly, lz):
    rows, far_y, far_z, corner, total = sizes(ny, nz, ly, lz)
    ry, fy = line_parts(ny * ly, RY)
    rz, fz = line_parts(nz * lz, RZ)
    ry, fy = ry.reshape(ny, ly), fy.reshape(ny, ly)
    rz, fz = rz.reshape(nz, lz), fz.reshape(nz, lz)
    ey = np.zeros((ny, ly, lz, total))
    ez = np.zeros((nz, ly, lz, total))
    for a in range(ny):
        block = line_block(ry[a], fy[a])
        ey[a, :, :, :rows] = np.repeat(block, lz, axis=1)[:, None, :]
        ey[a, :, :, far_y : far_y + lz] = fy[a][:, None, None]
        ey[a, :, :, far_y + lz : far_z] = ry[a][:, None, None]
        ey[a, :, :, far_z:corner] = np.tile(block, (1, nz))[:, None, :]
        ey[a, :, :, corner : corner + 2 * nz : 2] = fy[a][:, None, None]
        ey[a, :, :, corner + 1 : corner + 2 * nz : 2] = ry[a][:, None, None]
    for c in range(nz):
        block = line_block(rz[c], fz[c])
        ez[c, :, :, :far_z] = np.tile(block, (1, ly + 2))[None]
        for b in range(nz):
            weight = fz[c] if b < c else rz[c]
            if b != c:
                ez[c, :, :, far_z + b * ly : far_z + (b + 1) * ly] = weight[None, :, None]
                ez[c, :, :, corner + 2 * b : corner + 2 * b + 2] = weight[None, :, None]
    coef = np.concatenate([ry.reshape(-1), fy.reshape(-1)])
    zw = np.stack([rz, fz], axis=1)[..., None] * np.ones(LANES)
    f32 = lambda t: np.asarray(t, np.float32)
    return (
        f32(coef),
        f32(zw),
        f32(ey.reshape(ny, rows, total)),
        f32(ez.reshape(nz, rows, total)),
    )


def x_tables():
    q = decay(RX)
    i = np.arange(XB)
    toep = q ** np.abs(i[:, None] - i[None, :]) * q / (RX * (1.0 - q * q))
    toep = np.asarray(toep, np.float32)
    hi = toep.astype(jnp.bfloat16)
    lo = (toep - hi.astype(np.float32)).astype(jnp.bfloat16)
    uw = np.stack([q ** (i + 1.0), q ** (XB - i * 1.0)])[:, None, :] * np.ones((1, 8, 1))
    return np.stack([hi, lo]), np.asarray(uw, np.float32)


def split(x):
    hi = x.astype(jnp.bfloat16)
    return hi, (x - hi.astype(jnp.float32)).astype(jnp.bfloat16)


def dot(a, b):
    return jnp.dot(a, b, preferred_element_type=jnp.float32)


def dot3(a, b):
    return dot(a[0], b[0]) + (dot(a[1], b[0]) + dot(a[0], b[1]))


def kernel(
    ny, nz, owners,
    heat, speed, coef, zw, ey_hbm, ez_hbm, toep, uw,
    out,
    field, vel, zsend, zhalo, data, yface, zface, held, back, cface, chold, ey, ez,
    load_sem, hs_send, hs_recv, a_send, a_recv, b_send, b_recv, z_send, z_recv, c_send, c_recv,
):
    ly, lz, nx = heat.shape
    rows, far_y, far_z, corner, total = sizes(ny, nz, ly, lz)
    cw = nx // owners
    my = lax.axis_index("gy")
    mz = lax.axis_index("gz")

    loads = [
        pltpu.make_async_copy(heat, field.at[pl.ds(1, ly)], load_sem.at[0]),
        pltpu.make_async_copy(speed, vel, load_sem.at[1]),
        pltpu.make_async_copy(ey_hbm.at[my], ey, load_sem.at[2]),
        pltpu.make_async_copy(ez_hbm.at[mz], ez, load_sem.at[3]),
    ]
    for load in loads:
        load.start()

    barrier = pltpu.get_barrier_semaphore()
    for d in range(1, ny):
        pl.semaphore_signal(barrier, 1, device_id={"gy": lax.rem(my + d, ny)}, device_id_type=MESH)
    for d in range(1, nz):
        pl.semaphore_signal(barrier, 1, device_id={"gz": lax.rem(mz + d, nz)}, device_id_type=MESH)

    loads[0].wait()
    for y in range(ly):
        zsend[0, y : y + 1, :] = field[y + 1, 0:1, :]
        zsend[1, y : y + 1, :] = field[y + 1, lz - 1 : lz, :]
    pl.semaphore_wait(barrier, ny - 1 + nz - 1)

    def remote(src, dst, send, recv, target):
        return pltpu.make_async_remote_copy(
            src_ref=src, dst_ref=dst, send_sem=send, recv_sem=recv,
            device_id=target, device_id_type=MESH,
        )

    down_y = lax.rem(my + ny - 1, ny)
    up_y = lax.rem(my + 1, ny)
    down_z = lax.rem(mz + nz - 1, nz)
    up_z = lax.rem(mz + 1, nz)
    y_down = remote(field.at[1], field.at[ly + 1], hs_send.at[0], hs_recv.at[0], {"gy": down_y})
    y_up = remote(field.at[ly], field.at[0], hs_send.at[1], hs_recv.at[1], {"gy": up_y})
    z_down = remote(zsend.at[0], zhalo.at[1], hs_send.at[2], hs_recv.at[2], {"gz": down_z})
    z_up = remote(zsend.at[1], zhalo.at[0], hs_send.at[3], hs_recv.at[3], {"gz": up_z})
    first_y, last_y = my == 0, my == ny - 1
    first_z, last_z = mz == 0, mz == nz - 1

    @pl.when(jnp.logical_not(last_z))
    def _():
        z_up.start()

    @pl.when(jnp.logical_not(first_z))
    def _():
        z_down.start()

    @pl.when(jnp.logical_not(last_y))
    def _():
        y_up.start()

    @pl.when(jnp.logical_not(first_y))
    def _():
        y_down.start()

    @pl.when(first_y)
    def _():
        field[0] = jnp.zeros((lz, nx), jnp.float32)

    @pl.when(last_y)
    def _():
        field[ly + 1] = jnp.zeros((lz, nx), jnp.float32)

    @pl.when(first_z)
    def _():
        zhalo[0] = jnp.zeros((ly, nx), jnp.float32)

    @pl.when(last_z)
    def _():
        zhalo[1] = jnp.zeros((ly, nx), jnp.float32)

    data[pl.ds(pl.multiple_of(far_z + mz * ly, 8), ly), :] = jnp.zeros((ly, nx), jnp.float32)
    data[corner:total, :] = jnp.zeros((total - corner, nx), jnp.float32)
    for load in loads[1:]:
        load.wait()
    weights = split(ey[...] * ez[...])

    @pl.when(jnp.logical_not(first_y))
    def _():
        y_up.wait_recv()

    @pl.when(jnp.logical_not(last_y))
    def _():
        y_down.wait_recv()

    @pl.when(jnp.logical_not(first_z))
    def _():
        z_up.wait_recv()

    @pl.when(jnp.logical_not(last_z))
    def _():
        z_down.wait_recv()

    tile = lambda w: jnp.concatenate([w] * (nx // LANES), axis=1)
    rise_z = tile(zw[mz, 0])
    fall_z = tile(zw[mz, 1])
    level = lax.broadcasted_iota(jnp.int32, (lz, nx), 0)
    place = lax.broadcasted_iota(jnp.int32, (lz, nx), 1)
    yface[...] = jnp.zeros_like(yface)

    def layer(y, _):
        here = field[y + 1]
        south, north = field[y], field[y + 2]
        above = jnp.where(level == lz - 1, zhalo[1, pl.ds(y, 1), :], pltpu.roll(here, lz - 1, 0))
        below = jnp.where(level == 0, zhalo[0, pl.ds(y, 1), :], pltpu.roll(here, 1, 0))
        east = jnp.where(place == nx - 1, 0.0, pltpu.roll(here, nx - 1, 1))
        west = jnp.where(place == 0, 0.0, pltpu.roll(here, 1, 1))
        spread = east + west + north + south + above + below - 6.0 * here
        moved = (
            vel[0, y].astype(jnp.float32) * (east - west)
            + vel[1, y].astype(jnp.float32) * (north - south)
            + vel[2, y].astype(jnp.float32) * (above - below)
        )
        source = here + KAPPA * spread - 0.5 * moved
        data[pl.ds(pl.multiple_of(y * lz, lz), lz), :] = source
        yface[0:lz, :] += coef[my * ly + y] * source
        yface[lz : 2 * lz, :] += coef[ny * ly + my * ly + y] * source
        zface[0, pl.ds(y, 1), :] = jnp.sum(source * rise_z, axis=0, keepdims=True)
        zface[1, pl.ds(y, 1), :] = jnp.sum(source * fall_z, axis=0, keepdims=True)
        return 0

    lax.fori_loop(0, ly, layer, 0)

    def to_owner(owner):
        return remote(
            yface.at[:, pl.ds(pl.multiple_of(owner * cw, LANES), cw)], held.at[my],
            a_send.at[owner], a_recv.at[my], {"gy": owner},
        )

    def from_peer(peer):
        return remote(
            yface.at[:, pl.ds(0, cw)], held.at[peer], a_send.at[0], a_recv.at[peer], {"gy": peer}
        )

    def owned(index, body):
        if owners == ny:
            body()
        else:
            pl.when(index < owners)(body)

    for d in range(1, ny):
        peer = lax.rem(my + d, ny)
        owned(peer, lambda peer=peer: to_owner(peer).start())

    z_copies = []
    for d in range(1, nz):
        peer = lax.rem(mz + d, nz)
        side = (mz + d) // nz
        slot = data.at[pl.ds(pl.multiple_of(far_z + mz * ly, 8), ly)]
        copy = remote(zface.at[side], slot, z_send.at[peer], z_recv.at[mz], {"gz": peer})
        copy.start()
        z_copies.append(copy)

    def to_peer(peer):
        return remote(
            back.at[peer],
            data.at[pl.ds(far_y, 2 * lz), pl.ds(pl.multiple_of(my * cw, LANES), cw)],
            b_send.at[peer], b_recv.at[my], {"gy": peer},
        )

    def from_owner(owner):
        return remote(
            back.at[0],
            data.at[pl.ds(far_y, 2 * lz), pl.ds(pl.multiple_of(owner * cw, LANES), cw)],
            b_send.at[0], b_recv.at[owner], {"gy": owner},
        )

    def gather_sums():
        held[my] = yface[:, pl.ds(pl.multiple_of(my * cw, LANES), cw)]
        for d in range(1, ny):
            from_peer(lax.rem(my + d, ny)).wait_recv()
        run = jnp.zeros((lz, cw), jnp.float32)
        for a in range(ny):
            back[a, 0:lz, :] = run
            run = run + held[a, 0:lz, :]
        run = jnp.zeros((lz, cw), jnp.float32)
        for a in reversed(range(ny)):
            back[a, lz : 2 * lz, :] = run
            run = run + held[a, lz : 2 * lz, :]
        for d in range(1, ny):
            to_peer(lax.rem(my + d, ny)).start()
        data[far_y : far_y + 2 * lz, pl.ds(pl.multiple_of(my * cw, LANES), cw)] = back[my]

    owned(my, gather_sums)
    for d in range(1, ny):
        owner = lax.rem(my + d, ny)
        owned(owner, lambda owner=owner: from_owner(owner).wait_recv())

    for k in range(2):
        far = data[far_y + k * lz : far_y + (k + 1) * lz, :]
        cface[0, :, k * nx : (k + 1) * nx] = jnp.sum(far * rise_z, axis=0, keepdims=True)
        cface[1, :, k * nx : (k + 1) * nx] = jnp.sum(far * fall_z, axis=0, keepdims=True)
    c_copies = []
    for d in range(1, nz):
        peer = lax.rem(mz + d, nz)
        side = (mz + d) // nz
        copy = remote(cface.at[side], chold.at[mz], c_send.at[peer], c_recv.at[mz], {"gz": peer})
        copy.start()
        c_copies.append(copy)
    chold[mz] = jnp.zeros((1, 2 * nx), jnp.float32)
    for d in range(1, nz):
        peer = lax.rem(mz + d, nz)
        slot = data.at[pl.ds(pl.multiple_of(far_z + peer * ly, 8), ly)]
        remote(zface.at[0], slot, z_send.at[0], z_recv.at[peer], {"gz": peer}).wait_recv()
        remote(
            cface.at[0], chold.at[peer], c_send.at[0], c_recv.at[peer], {"gz": peer}
        ).wait_recv()
    for b in range(nz):
        for k in range(2):
            data[corner + 2 * b + k : corner + 2 * b + k + 1, :] = chold[b, :, k * nx : (k + 1) * nx]

    blocks = nx // XB
    toeplitz = (toep[0], toep[1])
    heads, tails = [], []
    for a in range(blocks):
        part = slice(a * XB, (a + 1) * XB)
        mixed = dot3(weights, split(data[:, part]))
        local = dot3(split(mixed), toeplitz)
        out[:, part] = local
        heads.append(local[:, 0:1])
        tails.append(local[:, XB - 1 : XB])
    q = decay(RX)
    step = float(q**XB)
    head, tail = heads[-1], tails[0]
    for a in range(1, blocks):
        tail = step * tail + tails[a]
        head = step * head + heads[blocks - 1 - a]
    scale = 1.0 / (1.0 - q ** (2.0 * nx + 2.0))
    near, far = float(-q * scale), float(q ** (nx + 2.0) * scale)
    ahead = [near * head + far * tail]
    after = [near * tail + far * head]
    for a in range(blocks - 1):
        ahead.append(step * ahead[-1] + tails[a])
        after.append(step * after[-1] + heads[blocks - 1 - a])
    after = after[::-1]
    grow, fade = uw[0, 0:1, :], uw[1, 0:1, :]
    for a in range(blocks):
        part = slice(a * XB, (a + 1) * XB)
        out[:, part] += ahead[a] * grow + after[a] * fade

    @pl.when(jnp.logical_not(last_z))
    def _():
        z_up.wait_send()

    @pl.when(jnp.logical_not(first_z))
    def _():
        z_down.wait_send()

    @pl.when(jnp.logical_not(last_y))
    def _():
        y_up.wait_send()

    @pl.when(jnp.logical_not(first_y))
    def _():
        y_down.wait_send()

    for d in range(1, ny):
        peer = lax.rem(my + d, ny)
        owned(peer, lambda peer=peer: to_owner(peer).wait_send())
    for copy in z_copies + c_copies:
        copy.wait_send()

    def sums_sent():
        for d in range(1, ny):
            to_peer(lax.rem(my + d, ny)).wait_send()

    owned(my, sums_sent)


def on_device(ny, nz, heat, speed):
    ly, lz, nx = heat.shape
    rows, far_y, far_z, corner, total = sizes(ny, nz, ly, lz)
    owners = min(ny, nx // LANES)
    while (nx // LANES) % owners:
        owners -= 1
    cw = nx // owners
    coef, zw, ey, ez = tables(ny, nz, ly, lz)
    toep, uw = x_tables()
    hbm = pl.BlockSpec(memory_space=pl.ANY)
    vmem = pl.BlockSpec(memory_space=pltpu.VMEM)
    smem = pl.BlockSpec(memory_space=pltpu.SMEM)
    dma = pltpu.SemaphoreType.DMA
    f32 = jnp.float32
    out = pl.pallas_call(
        functools.partial(kernel, ny, nz, owners),
        out_shape=jax.ShapeDtypeStruct((rows, nx), f32),
        in_specs=[hbm, hbm, smem, vmem, hbm, hbm, vmem, vmem],
        out_specs=vmem,
        scratch_shapes=[
            pltpu.VMEM((ly + 2, lz, nx), f32),
            pltpu.VMEM(speed.shape, speed.dtype),
            pltpu.VMEM((2, ly, nx), f32),
            pltpu.VMEM((2, ly, nx), f32),
            pltpu.VMEM((total, nx), f32),
            pltpu.VMEM((2 * lz, nx), f32),
            pltpu.VMEM((2, ly, nx), f32),
            pltpu.VMEM((ny, 2 * lz, cw), f32),
            pltpu.VMEM((ny, 2 * lz, cw), f32),
            pltpu.VMEM((2, 1, 2 * nx), f32),
            pltpu.VMEM((nz, 1, 2 * nx), f32),
            pltpu.VMEM((rows, total), f32),
            pltpu.VMEM((rows, total), f32),
            dma((4,)), dma((4,)), dma((4,)),
            dma((ny,)), dma((ny,)), dma((ny,)), dma((ny,)),
            dma((nz,)), dma((nz,)), dma((nz,)), dma((nz,)),
        ],
        compiler_params=pltpu.CompilerParams(
            collective_id=0, has_side_effects=True, vmem_limit_bytes=40 * 1024 * 1024
        ),
    )(heat, speed, jnp.asarray(coef), jnp.asarray(zw), jnp.asarray(ey), jnp.asarray(ez),
      jnp.asarray(toep), jnp.asarray(uw))
    return out.reshape(ly, lz, nx)


def solution(mesh):
    in_specs = (P("gy", "gz", None), P(None, "gy", "gz", None))
    return jax.shard_map(
        functools.partial(on_device, mesh.shape["gy"], mesh.shape["gz"]),
        mesh=mesh, in_specs=in_specs, out_specs=P("gy", "gz", None), check_vma=False,
    )
```

```python
import functools

import jax
import jax.numpy as jnp
import numpy as np
from jax import lax
from jax.experimental import pallas as pl
from jax.experimental.pallas import tpu as pltpu
from jax.sharding import PartitionSpec as P

RX = 1
RY = 768
RZ = 192
KAPPA = 0.15
XB = 256
LANES = 128
MESH = pl.DeviceIdType.MESH


def decay(ratio):
    h = 0.5 / ratio
    return 1.0 + h - np.sqrt(h * (2.0 + h))


def line_parts(n, ratio):
    q = decay(ratio)
    i = np.arange(n, dtype=np.float64)
    half = n / 2.0
    rise = q ** (-i + half) * (1.0 - q ** (2.0 * (i + 1.0)))
    fall = q ** (i + 1.0 - half) * (1.0 - q ** (2.0 * (n - i)))
    fall = fall / (ratio * (1.0 - q * q) * (1.0 - q ** (2.0 * n + 2.0)))
    return rise, fall


def line_block(rise, fall):
    n = len(rise)
    small = np.minimum(np.arange(n)[:, None], np.arange(n)[None, :])
    large = np.maximum(np.arange(n)[:, None], np.arange(n)[None, :])
    return rise[small] * fall[large]


def sizes(ny, nz, ly, lz):
    rows = ly * lz
    far_y = rows + nz * ly
    corner = far_y + 2 * lz
    total = corner + -(-2 * nz // 16) * 16
    return rows, far_y, corner, total


def tables(ny, nz, ly, lz):
    rows, far_y, corner, total = sizes(ny, nz, ly, lz)
    ry, fy = line_parts(ny * ly, RY)
    rz, fz = line_parts(nz * lz, RZ)
    ry, fy = ry.reshape(ny, ly), fy.reshape(ny, ly)
    rz, fz = rz.reshape(nz, lz), fz.reshape(nz, lz)
    ey = np.zeros((ny, ly, lz, total))
    ez = np.zeros((nz, ly, lz, total))
    for a in range(ny):
        block = line_block(ry[a], fy[a])
        ey[a, :, :, :rows] = np.repeat(block, lz, axis=1)[:, None, :]
        ey[a, :, :, rows:far_y] = np.tile(block, (1, nz))[:, None, :]
        ey[a, :, :, far_y : far_y + lz] = fy[a][:, None, None]
        ey[a, :, :, far_y + lz : corner] = ry[a][:, None, None]
        ey[a, :, :, corner : corner + 2 * nz : 2] = fy[a][:, None, None]
        ey[a, :, :, corner + 1 : corner + 2 * nz : 2] = ry[a][:, None, None]
    for c in range(nz):
        block = line_block(rz[c], fz[c])
        ez[c, :, :, :rows] = np.tile(block, (1, ly))[None]
        ez[c, :, :, far_y:corner] = np.tile(block, (1, 2))[None]
        for b in range(nz):
            weight = fz[c] if b < c else rz[c]
            if b != c:
                ez[c, :, :, rows + b * ly : rows + (b + 1) * ly] = weight[None, :, None]
                ez[c, :, :, corner + 2 * b : corner + 2 * b + 2] = weight[None, :, None]
    coef = np.concatenate([ry.reshape(-1), fy.reshape(-1)])
    zw = np.stack([rz, fz], axis=1)[..., None] * np.ones(LANES)
    f32 = lambda t: np.asarray(t, np.float32)
    return (
        f32(coef),
        f32(zw),
        f32(ey.reshape(ny, rows, total)),
        f32(ez.reshape(nz, rows, total)),
    )


def x_tables():
    q = decay(RX)
    i = np.arange(XB)
    toep = q ** np.abs(i[:, None] - i[None, :]) * q / (RX * (1.0 - q * q))
    toep = np.asarray(toep, np.float32)
    hi = toep.astype(jnp.bfloat16)
    lo = (toep - hi.astype(np.float32)).astype(jnp.bfloat16)
    uw = np.stack([q ** (i + 1.0), q ** (XB - i * 1.0)])[:, None, :] * np.ones((1, 8, 1))
    return np.stack([hi, lo]), np.asarray(uw, np.float32)


def split(x):
    hi = x.astype(jnp.bfloat16)
    return hi, (x - hi.astype(jnp.float32)).astype(jnp.bfloat16)


def dot(a, b):
    return jnp.dot(a, b, preferred_element_type=jnp.float32)


def dot3(a, b):
    return dot(a[0], b[0]) + (dot(a[1], b[0]) + dot(a[0], b[1]))


def dot_left(parts, x):
    hi, lo = split(x)
    return dot(parts, jnp.concatenate([hi, hi, lo], axis=0))


def left_parts(w):
    hi, lo = split(w)
    return jnp.concatenate([hi, lo, hi], axis=1)


def solve_x(pieces, toeplitz):
    blocks = len(pieces)
    rows = pieces[0].shape[0]
    hi, lo = split(jnp.concatenate(pieces, axis=0))
    local = dot(hi, toeplitz[0]) + (dot(lo, toeplitz[0]) + dot(hi, toeplitz[1]))
    return [local[a * rows : (a + 1) * rows] for a in range(blocks)]


def carries(heads, tails):
    blocks = len(heads)
    q = decay(RX)
    step = float(q**XB)
    nx = blocks * XB
    head, tail = heads[-1], tails[0]
    for a in range(1, blocks):
        tail = step * tail + tails[a]
        head = step * head + heads[blocks - 1 - a]
    scale = 1.0 / (1.0 - q ** (2.0 * nx + 2.0))
    near, far = float(-q * scale), float(q ** (nx + 2.0) * scale)
    ahead = [near * head + far * tail]
    after = [near * tail + far * head]
    for a in range(blocks - 1):
        ahead.append(step * ahead[-1] + tails[a])
        after.append(step * after[-1] + heads[blocks - 1 - a])
    return ahead, after[::-1]


def along_x(pieces, toeplitz, grow, fade):
    local = solve_x(pieces, toeplitz)
    ahead, after = carries([p[:, 0:1] for p in local], [p[:, XB - 1 : XB] for p in local])
    return [p + f * grow + g * fade for p, f, g in zip(local, ahead, after)]


def kernel(
    ny, nz, owners,
    heat, speed, coef_hbm, zw_hbm, ey_hbm, ez_hbm, toep_hbm, uw_hbm,
    out,
    field, vel, zsend, zhalo, data, far_z, far_y, corner_rows, mixed,
    yface, zface, held, back, cface, chold, coef, zw, ey, ez, toep, uw,
    load_sem, hs_send, hs_recv, a_send, a_recv, b_send, b_recv, z_send, z_recv, c_send, c_recv,
):
    ly, lz, nx = heat.shape
    rows, off_y, off_c, total = sizes(ny, nz, ly, lz)
    cw = nx // owners
    half = owners // 2
    blocks = nx // XB
    my = lax.axis_index("gy")
    mz = lax.axis_index("gz")
    inner = pl.ds(LANES, nx)

    loads = [
        pltpu.make_async_copy(heat, field.at[pl.ds(1, ly), :, inner], load_sem.at[0]),
        pltpu.make_async_copy(speed, vel, load_sem.at[1]),
        pltpu.make_async_copy(coef_hbm, coef, load_sem.at[2]),
        pltpu.make_async_copy(zw_hbm, zw, load_sem.at[3]),
        pltpu.make_async_copy(ey_hbm.at[my], ey, load_sem.at[4]),
        pltpu.make_async_copy(ez_hbm.at[mz], ez, load_sem.at[5]),
        pltpu.make_async_copy(toep_hbm, toep, load_sem.at[6]),
        pltpu.make_async_copy(uw_hbm, uw, load_sem.at[7]),
    ]
    loads[0].start()

    barrier = pltpu.get_barrier_semaphore()
    for d in range(1, ny):
        pl.semaphore_signal(barrier, 1, device_id={"gy": lax.rem(my + d, ny)}, device_id_type=MESH)
    for d in range(1, nz):
        pl.semaphore_signal(barrier, 1, device_id={"gz": lax.rem(mz + d, nz)}, device_id_type=MESH)
    for load in loads[1:]:
        load.start()

    first_y, last_y = my == 0, my == ny - 1
    first_z, last_z = mz == 0, mz == nz - 1
    edge = jnp.zeros((ly + 2, lz, LANES), jnp.float32)
    field[:, :, 0:LANES] = edge
    field[:, :, LANES + nx : 2 * LANES + nx] = edge

    @pl.when(first_y)
    def _():
        field[0, :, inner] = jnp.zeros((lz, nx), jnp.float32)

    @pl.when(last_y)
    def _():
        field[ly + 1, :, inner] = jnp.zeros((lz, nx), jnp.float32)

    @pl.when(first_z)
    def _():
        zhalo[0] = jnp.zeros((ly, nx), jnp.float32)

    @pl.when(last_z)
    def _():
        zhalo[1] = jnp.zeros((ly, nx), jnp.float32)

    far_z[pl.ds(pl.multiple_of(mz * ly, 8), ly), :] = jnp.zeros((ly, nx), jnp.float32)
    corner_rows[...] = jnp.zeros_like(corner_rows)
    chold[mz] = jnp.zeros((1, 2 * nx), jnp.float32)

    loads[0].wait()
    for y in range(ly):
        zsend[0, y : y + 1, :] = field[y + 1, 0:1, inner]
        zsend[1, y : y + 1, :] = field[y + 1, lz - 1 : lz, inner]
    pl.semaphore_wait(barrier, ny - 1 + nz - 1)

    def remote(src, dst, send, recv, target):
        return pltpu.make_async_remote_copy(
            src_ref=src, dst_ref=dst, send_sem=send, recv_sem=recv,
            device_id=target, device_id_type=MESH,
        )

    down_y = lax.rem(my + ny - 1, ny)
    up_y = lax.rem(my + 1, ny)
    down_z = lax.rem(mz + nz - 1, nz)
    up_z = lax.rem(mz + 1, nz)
    y_down = remote(
        field.at[1, :, inner], field.at[ly + 1, :, inner],
        hs_send.at[0], hs_recv.at[0], {"gy": down_y},
    )
    y_up = remote(
        field.at[ly, :, inner], field.at[0, :, inner],
        hs_send.at[1], hs_recv.at[1], {"gy": up_y},
    )
    z_down = remote(zsend.at[0], zhalo.at[1], hs_send.at[2], hs_recv.at[2], {"gz": down_z})
    z_up = remote(zsend.at[1], zhalo.at[0], hs_send.at[3], hs_recv.at[3], {"gz": up_z})
    has_below = (
        (jnp.logical_not(first_y), y_down, y_up), (jnp.logical_not(first_z), z_down, z_up)
    )
    has_above = ((jnp.logical_not(last_y), y_up, y_down), (jnp.logical_not(last_z), z_up, z_down))
    ends = has_below + has_above
    for there, sent, _ in ends:
        pl.when(there)(lambda sent=sent: sent.start())

    for load in loads[1:]:
        load.wait()
    weights = ey[...] * ez[...]
    w_own = split(weights[:, :rows])
    w_z = left_parts(weights[:, rows:off_y])
    w_y = left_parts(weights[:, off_y:off_c])
    w_c = left_parts(weights[:, off_c:total])
    toeplitz = (toep[0], toep[1])
    grow, fade = uw[0, 0:1, :], uw[1, 0:1, :]

    for there, _, received in ends:
        pl.when(there)(lambda received=received: received.wait_recv())

    def column(owner):
        if owners % 2 or owners == 1:
            return pl.multiple_of(owner * cw, LANES)
        block = jnp.where(owner < half, 2 * owner, 2 * (owners - 1 - owner) + 1)
        return pl.multiple_of(block * cw, LANES)

    def owner_of(block):
        if owners % 2 or owners == 1:
            return block
        return block // 2 if block % 2 == 0 else owners - 1 - block // 2

    def to_owner(owner):
        return remote(
            yface.at[:, pl.ds(column(owner), cw)], held.at[my],
            a_send.at[owner], a_recv.at[my], {"gy": owner},
        )

    def from_peer(peer):
        return remote(
            yface.at[:, pl.ds(0, cw)], held.at[peer], a_send.at[0], a_recv.at[peer], {"gy": peer}
        )

    def owned(index, body):
        if owners == ny:
            body()
        else:
            pl.when(index < owners)(body)

    chunk = 512
    tile = lambda w: jnp.concatenate([w] * (chunk // LANES), axis=1)
    rise_z = tile(zw[mz, 0])
    fall_z = tile(zw[mz, 1])
    level = lax.broadcasted_iota(jnp.int32, (lz, chunk), 0)
    wide = chunk + 2 * LANES

    for x in range(0, nx, chunk):
        cols = pl.ds(x, chunk)
        mid = pl.ds(x + LANES, chunk)

        def layer(y, sums, x=x, cols=cols, mid=mid):
            window = field[y + 1, :, pl.ds(x, wide)]
            here = window[:, LANES : LANES + chunk]
            east = pltpu.roll(window, wide - 1, 1)[:, LANES : LANES + chunk]
            west = pltpu.roll(window, 1, 1)[:, LANES : LANES + chunk]
            south, north = field[y, :, mid], field[y + 2, :, mid]
            row = pl.ds(y, 1)
            above = jnp.where(level == lz - 1, zhalo[1, row, cols], pltpu.roll(here, lz - 1, 0))
            below = jnp.where(level == 0, zhalo[0, row, cols], pltpu.roll(here, 1, 0))
            spread = (east + west) + (north + south) + (above + below)
            moved = (
                vel[0, y, :, cols].astype(jnp.float32) * (east - west)
                + vel[1, y, :, cols].astype(jnp.float32) * (north - south)
                + vel[2, y, :, cols].astype(jnp.float32) * (above - below)
            )
            source = (1.0 - 6.0 * KAPPA) * here + KAPPA * spread - 0.5 * moved
            data[pl.ds(pl.multiple_of(y * lz, lz), lz), cols] = source
            zface[0, row, cols] = jnp.sum(source * rise_z, axis=0, keepdims=True)
            zface[1, row, cols] = jnp.sum(source * fall_z, axis=0, keepdims=True)
            place = my * ly + y
            return (sums[0] + coef[place] * source, sums[1] + coef[ny * ly + place] * source)

        zero = jnp.zeros((lz, chunk), jnp.float32)
        rising, falling = lax.fori_loop(0, ly, layer, (zero, zero), unroll=4)
        yface[0:lz, cols] = rising
        yface[lz : 2 * lz, cols] = falling
        for block in range(x // cw, (x + chunk) // cw):
            owner = owner_of(block)
            pl.when(my != owner)(lambda owner=owner: to_owner(owner).start())

    z_copies = []
    for d in range(1, nz):
        peer = lax.rem(mz + d, nz)
        side = (mz + d) // nz
        slot = far_z.at[pl.ds(pl.multiple_of(mz * ly, 8), ly)]
        copy = remote(zface.at[side], slot, z_send.at[peer], z_recv.at[mz], {"gz": peer})
        copy.start()
        z_copies.append(copy)

    parts = [slice(a * XB, (a + 1) * XB) for a in range(blocks)]
    for part in parts:
        mixed[:, part] = dot3(w_own, split(data[:, part]))

    def to_peer(peer):
        return remote(
            back.at[peer], far_y.at[:, pl.ds(column(my), cw)],
            b_send.at[peer], b_recv.at[my], {"gy": peer},
        )

    def from_owner(owner):
        return remote(
            back.at[0], far_y.at[:, pl.ds(column(owner), cw)],
            b_send.at[0], b_recv.at[owner], {"gy": owner},
        )

    def gather_sums():
        held[my] = yface[:, pl.ds(column(my), cw)]
        for d in range(1, ny):
            from_peer(lax.rem(my + d, ny)).wait_recv()
        run = jnp.zeros((lz, cw), jnp.float32)
        for a in range(ny):
            back[a, 0:lz, :] = run
            run = run + held[a, 0:lz, :]
        run = jnp.zeros((lz, cw), jnp.float32)
        for a in reversed(range(ny)):
            back[a, lz : 2 * lz, :] = run
            run = run + held[a, lz : 2 * lz, :]
        for d in range(1, ny):
            to_peer(lax.rem(my + d, ny)).start()
        far_y[:, pl.ds(column(my), cw)] = back[my]

    owned(my, gather_sums)

    for d in range(1, nz):
        peer = lax.rem(mz + d, nz)
        slot = far_z.at[pl.ds(pl.multiple_of(peer * ly, 8), ly)]
        remote(zface.at[0], slot, z_send.at[0], z_recv.at[peer], {"gz": peer}).wait_recv()
    heads, tails = [], []
    for part in parts:
        both = mixed[:, part] + dot_left(w_z, far_z[:, part])
        local = dot3(split(both), toeplitz)
        out[:, part] = local
        heads.append(local[:, 0:1])
        tails.append(local[:, XB - 1 : XB])
    ahead, after = carries(heads, tails)
    for part, f, g in zip(parts, ahead, after):
        out[:, part] += f * grow + g * fade

    for d in range(1, ny):
        owner = lax.rem(my + d, ny)
        owned(owner, lambda owner=owner: from_owner(owner).wait_recv())

    whole = lambda w: jnp.concatenate([w] * (nx // LANES), axis=1)
    for side in range(2):
        weight = whole(zw[mz, side])
        for k in range(2):
            far = far_y[k * lz : (k + 1) * lz, :]
            cface[side, :, k * nx : (k + 1) * nx] = jnp.sum(far * weight, axis=0, keepdims=True)
    c_copies = []
    for d in range(1, nz):
        peer = lax.rem(mz + d, nz)
        side = (mz + d) // nz
        copy = remote(cface.at[side], chold.at[mz], c_send.at[peer], c_recv.at[mz], {"gz": peer})
        copy.start()
        c_copies.append(copy)

    solved = along_x([far_y[:, part] for part in parts], toeplitz, grow, fade)
    for part, piece in zip(parts, solved):
        out[:, part] += dot_left(w_y, piece)

    for d in range(1, nz):
        peer = lax.rem(mz + d, nz)
        remote(
            cface.at[0], chold.at[peer], c_send.at[0], c_recv.at[peer], {"gz": peer}
        ).wait_recv()
    for b in range(nz):
        for k in range(2):
            corner_rows[2 * b + k : 2 * b + k + 1, :] = chold[b, :, k * nx : (k + 1) * nx]
    solved = along_x([corner_rows[:, part] for part in parts], toeplitz, grow, fade)
    for part, piece in zip(parts, solved):
        out[:, part] += dot_left(w_c, piece)

    for there, sent, _ in ends:
        pl.when(there)(lambda sent=sent: sent.wait_send())
    for block in range(owners):
        owner = owner_of(block)
        pl.when(my != owner)(lambda owner=owner: to_owner(owner).wait_send())
    for copy in z_copies + c_copies:
        copy.wait_send()

    def sums_sent():
        for d in range(1, ny):
            to_peer(lax.rem(my + d, ny)).wait_send()

    owned(my, sums_sent)


def on_device(ny, nz, heat, speed):
    ly, lz, nx = heat.shape
    rows, far_y, corner, total = sizes(ny, nz, ly, lz)
    owners = min(ny, nx // LANES)
    while (nx // LANES) % owners:
        owners -= 1
    cw = nx // owners
    coef, zw, ey, ez = tables(ny, nz, ly, lz)
    toep, uw = x_tables()
    hbm = pl.BlockSpec(memory_space=pltpu.HBM)
    vmem = pl.BlockSpec(memory_space=pltpu.VMEM)
    dma = pltpu.SemaphoreType.DMA
    f32 = jnp.float32
    out = pl.pallas_call(
        functools.partial(kernel, ny, nz, owners),
        out_shape=jax.ShapeDtypeStruct((rows, nx), f32),
        in_specs=[hbm] * 8,
        out_specs=vmem,
        scratch_shapes=[
            pltpu.VMEM((ly + 2, lz, nx + 2 * LANES), f32),
            pltpu.VMEM(speed.shape, speed.dtype),
            pltpu.VMEM((2, ly, nx), f32),
            pltpu.VMEM((2, ly, nx), f32),
            pltpu.VMEM((rows, nx), f32),
            pltpu.VMEM((nz * ly, nx), f32),
            pltpu.VMEM((2 * lz, nx), f32),
            pltpu.VMEM((total - corner, nx), f32),
            pltpu.VMEM((rows, nx), f32),
            pltpu.VMEM((2 * lz, nx), f32),
            pltpu.VMEM((2, ly, nx), f32),
            pltpu.VMEM((ny, 2 * lz, cw), f32),
            pltpu.VMEM((ny, 2 * lz, cw), f32),
            pltpu.VMEM((2, 1, 2 * nx), f32),
            pltpu.VMEM((nz, 1, 2 * nx), f32),
            pltpu.SMEM(coef.shape, f32),
            pltpu.VMEM(zw.shape, f32),
            pltpu.VMEM((rows, total), f32),
            pltpu.VMEM((rows, total), f32),
            pltpu.VMEM(toep.shape, jnp.bfloat16),
            pltpu.VMEM(uw.shape, f32),
            dma((8,)), dma((4,)), dma((4,)),
            dma((ny,)), dma((ny,)), dma((ny,)), dma((ny,)),
            dma((nz,)), dma((nz,)), dma((nz,)), dma((nz,)),
        ],
        compiler_params=pltpu.CompilerParams(
            collective_id=0, has_side_effects=True, vmem_limit_bytes=40 * 1024 * 1024
        ),
    )(heat, speed, jnp.asarray(coef), jnp.asarray(zw), jnp.asarray(ey), jnp.asarray(ez),
      jnp.asarray(toep), jnp.asarray(uw))
    return out.reshape(ly, lz, nx)


def solution(mesh):
    in_specs = (P("gy", "gz", None), P(None, "gy", "gz", None))
    return jax.shard_map(
        functools.partial(on_device, mesh.shape["gy"], mesh.shape["gz"]),
        mesh=mesh, in_specs=in_specs, out_specs=P("gy", "gz", None), check_vma=False,
    )
```

```python
import functools

import jax
import jax.numpy as jnp
import numpy as np
from jax import lax
from jax.experimental import pallas as pl
from jax.experimental.pallas import tpu as pltpu
from jax.sharding import PartitionSpec as P

RX = 1
RY = 768
RZ = 192
KAPPA = 0.15
XB = 256
LANES = 128
MESH = pl.DeviceIdType.MESH


def decay(ratio):
    h = 0.5 / ratio
    return 1.0 + h - np.sqrt(h * (2.0 + h))


def line_parts(n, ratio):
    q = decay(ratio)
    i = np.arange(n, dtype=np.float64)
    half = n / 2.0
    rise = q ** (-i + half) * (1.0 - q ** (2.0 * (i + 1.0)))
    fall = q ** (i + 1.0 - half) * (1.0 - q ** (2.0 * (n - i)))
    fall = fall / (ratio * (1.0 - q * q) * (1.0 - q ** (2.0 * n + 2.0)))
    return rise, fall


def line_block(rise, fall):
    n = len(rise)
    small = np.minimum(np.arange(n)[:, None], np.arange(n)[None, :])
    large = np.maximum(np.arange(n)[:, None], np.arange(n)[None, :])
    return rise[small] * fall[large]


def sizes(ny, nz, ly, lz):
    rows = ly * lz
    far_y = rows + nz * ly
    corner = far_y + 2 * lz
    total = corner + -(-2 * nz // 16) * 16
    return rows, far_y, corner, total


def tables(ny, nz, ly, lz):
    rows, far_y, corner, total = sizes(ny, nz, ly, lz)
    ry, fy = line_parts(ny * ly, RY)
    rz, fz = line_parts(nz * lz, RZ)
    ry, fy = ry.reshape(ny, ly), fy.reshape(ny, ly)
    rz, fz = rz.reshape(nz, lz), fz.reshape(nz, lz)
    ey = np.zeros((ny, ly, lz, total))
    ez = np.zeros((nz, ly, lz, total))
    for a in range(ny):
        block = line_block(ry[a], fy[a])
        ey[a, :, :, :rows] = np.repeat(block, lz, axis=1)[:, None, :]
        ey[a, :, :, rows:far_y] = np.tile(block, (1, nz))[:, None, :]
        ey[a, :, :, far_y : far_y + lz] = fy[a][:, None, None]
        ey[a, :, :, far_y + lz : corner] = ry[a][:, None, None]
        ey[a, :, :, corner : corner + 2 * nz : 2] = fy[a][:, None, None]
        ey[a, :, :, corner + 1 : corner + 2 * nz : 2] = ry[a][:, None, None]
    for c in range(nz):
        block = line_block(rz[c], fz[c])
        ez[c, :, :, :rows] = np.tile(block, (1, ly))[None]
        ez[c, :, :, far_y:corner] = np.tile(block, (1, 2))[None]
        for b in range(nz):
            weight = fz[c] if b < c else rz[c]
            if b != c:
                ez[c, :, :, rows + b * ly : rows + (b + 1) * ly] = weight[None, :, None]
                ez[c, :, :, corner + 2 * b : corner + 2 * b + 2] = weight[None, :, None]
    coef = np.concatenate([ry.reshape(-1), fy.reshape(-1)])
    zw = np.stack([rz, fz], axis=1)[..., None] * np.ones(LANES)
    f32 = lambda t: np.asarray(t, np.float32)
    return (
        f32(coef),
        f32(zw),
        f32(ey.reshape(ny, rows, total)),
        f32(ez.reshape(nz, rows, total)),
    )


def x_tables():
    q = decay(RX)
    i = np.arange(XB)
    toep = q ** np.abs(i[:, None] - i[None, :]) * q / (RX * (1.0 - q * q))
    toep = np.asarray(toep, np.float32)
    hi = toep.astype(jnp.bfloat16)
    lo = (toep - hi.astype(np.float32)).astype(jnp.bfloat16)
    uw = np.stack([q ** (i + 1.0), q ** (XB - i * 1.0)])[:, None, :] * np.ones((1, 8, 1))
    return np.stack([hi, lo]), np.asarray(uw, np.float32)


def split(x):
    hi = x.astype(jnp.bfloat16)
    return hi, (x - hi.astype(jnp.float32)).astype(jnp.bfloat16)


def dot(a, b):
    return jnp.dot(a, b, preferred_element_type=jnp.float32)


def dot3(a, b):
    return dot(a[0], b[0]) + (dot(a[1], b[0]) + dot(a[0], b[1]))


def dot_left(parts, x):
    hi, lo = split(x)
    return dot(parts, jnp.concatenate([hi, hi, lo], axis=0))


def left_parts(w):
    hi, lo = split(w)
    return jnp.concatenate([hi, lo, hi], axis=1)


def solve_x(pieces, toeplitz):
    blocks = len(pieces)
    rows = pieces[0].shape[0]
    hi, lo = split(jnp.concatenate(pieces, axis=0))
    local = dot(hi, toeplitz[0]) + (dot(lo, toeplitz[0]) + dot(hi, toeplitz[1]))
    return [local[a * rows : (a + 1) * rows] for a in range(blocks)]


def carries(heads, tails):
    blocks = len(heads)
    q = decay(RX)
    step = float(q**XB)
    nx = blocks * XB
    head, tail = heads[-1], tails[0]
    for a in range(1, blocks):
        tail = step * tail + tails[a]
        head = step * head + heads[blocks - 1 - a]
    scale = 1.0 / (1.0 - q ** (2.0 * nx + 2.0))
    near, far = float(-q * scale), float(q ** (nx + 2.0) * scale)
    ahead = [near * head + far * tail]
    after = [near * tail + far * head]
    for a in range(blocks - 1):
        ahead.append(step * ahead[-1] + tails[a])
        after.append(step * after[-1] + heads[blocks - 1 - a])
    return ahead, after[::-1]


def along_x(pieces, toeplitz, grow, fade):
    local = solve_x(pieces, toeplitz)
    ahead, after = carries([p[:, 0:1] for p in local], [p[:, XB - 1 : XB] for p in local])
    return [p + f * grow + g * fade for p, f, g in zip(local, ahead, after)]


def kernel(
    ny, nz, owners,
    heat, speed, coef_hbm, zw_hbm, ey_hbm, ez_hbm, toep_hbm, uw_hbm,
    out,
    field, vel, zsend, zhalo, data, far_z, far_y, corner_rows, mixed, acc,
    yface, zface, held, back, cface, chold, coef, zw, ey, ez, toep, uw,
    load_sem, out_sem, hs_send, hs_recv, a_send, a_recv, b_send, b_recv, z_send, z_recv, c_send, c_recv,
):
    ly, lz, nx = heat.shape
    rows, off_y, off_c, total = sizes(ny, nz, ly, lz)
    cw = nx // owners
    half = owners // 2
    blocks = nx // XB
    my = lax.axis_index("gy")
    mz = lax.axis_index("gz")
    inner = pl.ds(LANES, nx)

    loads = [
        pltpu.make_async_copy(heat, field.at[pl.ds(1, ly), :, inner], load_sem.at[0]),
        pltpu.make_async_copy(speed, vel, load_sem.at[1]),
        pltpu.make_async_copy(coef_hbm, coef, load_sem.at[2]),
        pltpu.make_async_copy(zw_hbm, zw, load_sem.at[3]),
        pltpu.make_async_copy(ey_hbm.at[my], ey, load_sem.at[4]),
        pltpu.make_async_copy(ez_hbm.at[mz], ez, load_sem.at[5]),
        pltpu.make_async_copy(toep_hbm, toep, load_sem.at[6]),
        pltpu.make_async_copy(uw_hbm, uw, load_sem.at[7]),
    ]
    loads[0].start()

    barrier = pltpu.get_barrier_semaphore()
    for d in range(1, ny):
        pl.semaphore_signal(barrier, 1, device_id={"gy": lax.rem(my + d, ny)}, device_id_type=MESH)
    for d in range(1, nz):
        pl.semaphore_signal(barrier, 1, device_id={"gz": lax.rem(mz + d, nz)}, device_id_type=MESH)
    for load in loads[1:]:
        load.start()

    first_y, last_y = my == 0, my == ny - 1
    first_z, last_z = mz == 0, mz == nz - 1
    edge = jnp.zeros((ly + 2, lz, LANES), jnp.float32)
    field[:, :, 0:LANES] = edge
    field[:, :, LANES + nx : 2 * LANES + nx] = edge

    @pl.when(first_y)
    def _():
        field[0, :, inner] = jnp.zeros((lz, nx), jnp.float32)

    @pl.when(last_y)
    def _():
        field[ly + 1, :, inner] = jnp.zeros((lz, nx), jnp.float32)

    @pl.when(first_z)
    def _():
        zhalo[0] = jnp.zeros((ly, nx), jnp.float32)

    @pl.when(last_z)
    def _():
        zhalo[1] = jnp.zeros((ly, nx), jnp.float32)

    far_z[pl.ds(pl.multiple_of(mz * ly, 8), ly), :] = jnp.zeros((ly, nx), jnp.float32)
    corner_rows[...] = jnp.zeros_like(corner_rows)
    chold[mz] = jnp.zeros((1, 2 * nx), jnp.float32)

    loads[0].wait()
    for y in range(ly):
        zsend[0, y : y + 1, :] = field[y + 1, 0:1, inner]
        zsend[1, y : y + 1, :] = field[y + 1, lz - 1 : lz, inner]
    pl.semaphore_wait(barrier, ny - 1 + nz - 1)

    def remote(src, dst, send, recv, target):
        return pltpu.make_async_remote_copy(
            src_ref=src, dst_ref=dst, send_sem=send, recv_sem=recv,
            device_id=target, device_id_type=MESH,
        )

    down_y = lax.rem(my + ny - 1, ny)
    up_y = lax.rem(my + 1, ny)
    down_z = lax.rem(mz + nz - 1, nz)
    up_z = lax.rem(mz + 1, nz)
    chunk = 512
    chunks = nx // chunk
    inside = (
        (jnp.logical_not(first_y), jnp.logical_not(last_y)),
        (jnp.logical_not(first_z), jnp.logical_not(last_z)),
    )
    ends = []
    for n in range(chunks):
        cols = pl.ds(n * chunk, chunk)
        mid = pl.ds(n * chunk + LANES, chunk)
        y_down = remote(
            field.at[1, :, mid], field.at[ly + 1, :, mid],
            hs_send.at[0, n], hs_recv.at[0, n], {"gy": down_y},
        )
        y_up = remote(
            field.at[ly, :, mid], field.at[0, :, mid],
            hs_send.at[1, n], hs_recv.at[1, n], {"gy": up_y},
        )
        z_down = remote(
            zsend.at[0, :, cols], zhalo.at[1, :, cols],
            hs_send.at[2, n], hs_recv.at[2, n], {"gz": down_z},
        )
        z_up = remote(
            zsend.at[1, :, cols], zhalo.at[0, :, cols],
            hs_send.at[3, n], hs_recv.at[3, n], {"gz": up_z},
        )
        ends.append((
            (inside[0][0], y_down, y_up), (inside[0][1], y_up, y_down),
            (inside[1][0], z_down, z_up), (inside[1][1], z_up, z_down),
        ))
    for end in ends:
        for there, sent, _ in end:
            pl.when(there)(lambda sent=sent: sent.start())

    for load in loads[1:]:
        load.wait()
    weights = ey[...] * ez[...]
    w_own = split(weights[:, :rows])
    w_z = left_parts(weights[:, rows:off_y])
    w_y = left_parts(weights[:, off_y:off_c])
    w_c = left_parts(weights[:, off_c:total])
    toeplitz = (toep[0], toep[1])
    grow, fade = uw[0, 0:1, :], uw[1, 0:1, :]

    def column(owner):
        if owners % 2 or owners == 1:
            return pl.multiple_of(owner * cw, LANES)
        block = jnp.where(owner < half, 2 * owner, 2 * (owners - 1 - owner) + 1)
        return pl.multiple_of(block * cw, LANES)

    def owner_of(block):
        if owners % 2 or owners == 1:
            return block
        return block // 2 if block % 2 == 0 else owners - 1 - block // 2

    def to_owner(owner):
        return remote(
            yface.at[:, pl.ds(column(owner), cw)], held.at[my],
            a_send.at[owner], a_recv.at[my], {"gy": owner},
        )

    def from_peer(peer):
        return remote(
            yface.at[:, pl.ds(0, cw)], held.at[peer], a_send.at[0], a_recv.at[peer], {"gy": peer}
        )

    def owned(index, body):
        if owners == ny:
            body()
        else:
            pl.when(index < owners)(body)

    tile = lambda w: jnp.concatenate([w] * (chunk // LANES), axis=1)
    rise_z = tile(zw[mz, 0])
    fall_z = tile(zw[mz, 1])
    level = lax.broadcasted_iota(jnp.int32, (lz, chunk), 0)
    wide = chunk + 2 * LANES

    z_copies = []
    for x in range(0, nx, chunk):
        for there, _, received in ends[x // chunk]:
            pl.when(there)(lambda received=received: received.wait_recv())
        cols = pl.ds(x, chunk)
        mid = pl.ds(x + LANES, chunk)

        def layer(y, sums, x=x, cols=cols, mid=mid):
            window = field[y + 1, :, pl.ds(x, wide)]
            here = window[:, LANES : LANES + chunk]
            east = pltpu.roll(window, wide - 1, 1)[:, LANES : LANES + chunk]
            west = pltpu.roll(window, 1, 1)[:, LANES : LANES + chunk]
            south, north = field[y, :, mid], field[y + 2, :, mid]
            row = pl.ds(y, 1)
            above = jnp.where(level == lz - 1, zhalo[1, row, cols], pltpu.roll(here, lz - 1, 0))
            below = jnp.where(level == 0, zhalo[0, row, cols], pltpu.roll(here, 1, 0))
            spread = (east + west) + (north + south) + (above + below)
            moved = (
                vel[0, y, :, cols].astype(jnp.float32) * (east - west)
                + vel[1, y, :, cols].astype(jnp.float32) * (north - south)
                + vel[2, y, :, cols].astype(jnp.float32) * (above - below)
            )
            source = (1.0 - 6.0 * KAPPA) * here + KAPPA * spread - 0.5 * moved
            data[pl.ds(pl.multiple_of(y * lz, lz), lz), cols] = source
            zface[0, row, cols] = jnp.sum(source * rise_z, axis=0, keepdims=True)
            zface[1, row, cols] = jnp.sum(source * fall_z, axis=0, keepdims=True)
            place = my * ly + y
            return (sums[0] + coef[place] * source, sums[1] + coef[ny * ly + place] * source)

        zero = jnp.zeros((lz, chunk), jnp.float32)
        rising, falling = lax.fori_loop(0, ly, layer, (zero, zero), unroll=4)
        yface[0:lz, cols] = rising
        yface[lz : 2 * lz, cols] = falling
        for block in range(x // cw, (x + chunk) // cw):
            owner = owner_of(block)
            pl.when(my != owner)(lambda owner=owner: to_owner(owner).start())

        for d in range(1, nz):
            peer = lax.rem(mz + d, nz)
            side = (mz + d) // nz
            slot = far_z.at[pl.ds(pl.multiple_of(mz * ly, 8), ly), cols]
            n = x // chunk
            copy = remote(
                zface.at[side, :, cols], slot, z_send.at[peer, n], z_recv.at[mz, n], {"gz": peer}
            )
            copy.start()
            z_copies.append(copy)

    parts = [slice(a * XB, (a + 1) * XB) for a in range(blocks)]
    for part in parts:
        mixed[:, part] = dot3(w_own, split(data[:, part]))

    def to_peer(peer):
        return remote(
            back.at[peer], far_y.at[:, pl.ds(column(my), cw)],
            b_send.at[peer], b_recv.at[my], {"gy": peer},
        )

    def from_owner(owner):
        return remote(
            back.at[0], far_y.at[:, pl.ds(column(owner), cw)],
            b_send.at[0], b_recv.at[owner], {"gy": owner},
        )

    def gather_sums():
        held[my] = yface[:, pl.ds(column(my), cw)]
        for d in range(1, ny):
            from_peer(lax.rem(my + d, ny)).wait_recv()
        run = jnp.zeros((lz, cw), jnp.float32)
        for a in range(ny):
            back[a, 0:lz, :] = run
            run = run + held[a, 0:lz, :]
        run = jnp.zeros((lz, cw), jnp.float32)
        for a in reversed(range(ny)):
            back[a, lz : 2 * lz, :] = run
            run = run + held[a, lz : 2 * lz, :]
        for d in range(1, ny):
            to_peer(lax.rem(my + d, ny)).start()
        far_y[:, pl.ds(column(my), cw)] = back[my]

    owned(my, gather_sums)

    for d in range(1, nz):
        peer = lax.rem(mz + d, nz)
        for n in range(chunks):
            cols = pl.ds(n * chunk, chunk)
            slot = far_z.at[pl.ds(pl.multiple_of(peer * ly, 8), ly), cols]
            remote(
                zface.at[0, :, cols], slot, z_send.at[0, n], z_recv.at[peer, n], {"gz": peer}
            ).wait_recv()
    both = [mixed[:, part] + dot_left(w_z, far_z[:, part]) for part in parts]
    for part, piece in zip(parts, along_x(both, toeplitz, grow, fade)):
        acc[:, part] = piece

    for d in range(1, ny):
        owner = lax.rem(my + d, ny)
        owned(owner, lambda owner=owner: from_owner(owner).wait_recv())

    whole = lambda w: jnp.concatenate([w] * (nx // LANES), axis=1)
    for side in range(2):
        weight = whole(zw[mz, side])
        for k in range(2):
            far = far_y[k * lz : (k + 1) * lz, :]
            cface[side, :, k * nx : (k + 1) * nx] = jnp.sum(far * weight, axis=0, keepdims=True)
    c_copies = []
    for d in range(1, nz):
        peer = lax.rem(mz + d, nz)
        side = (mz + d) // nz
        copy = remote(cface.at[side], chold.at[mz], c_send.at[peer], c_recv.at[mz], {"gz": peer})
        copy.start()
        c_copies.append(copy)

    solved = along_x([far_y[:, part] for part in parts], toeplitz, grow, fade)
    for part, piece in zip(parts, solved):
        acc[:, part] += dot_left(w_y, piece)

    for d in range(1, nz):
        peer = lax.rem(mz + d, nz)
        remote(
            cface.at[0], chold.at[peer], c_send.at[0], c_recv.at[peer], {"gz": peer}
        ).wait_recv()
    for b in range(nz):
        for k in range(2):
            corner_rows[2 * b + k : 2 * b + k + 1, :] = chold[b, :, k * nx : (k + 1) * nx]
    solved = along_x([corner_rows[:, part] for part in parts], toeplitz, grow, fade)
    stores = []
    for a, (part, piece) in enumerate(zip(parts, solved)):
        acc[:, part] += dot_left(w_c, piece)
        place = pl.ds(a * XB, XB)
        stores.append(pltpu.make_async_copy(acc.at[:, place], out.at[:, place], out_sem.at[a]))
        stores[-1].start()

    for end in ends:
        for there, sent, _ in end:
            pl.when(there)(lambda sent=sent: sent.wait_send())
    for block in range(owners):
        owner = owner_of(block)
        pl.when(my != owner)(lambda owner=owner: to_owner(owner).wait_send())
    for copy in z_copies + c_copies:
        copy.wait_send()

    def sums_sent():
        for d in range(1, ny):
            to_peer(lax.rem(my + d, ny)).wait_send()

    owned(my, sums_sent)
    for store in stores:
        store.wait()


def on_device(ny, nz, heat, speed):
    ly, lz, nx = heat.shape
    rows, far_y, corner, total = sizes(ny, nz, ly, lz)
    owners = min(ny, nx // LANES)
    while (nx // LANES) % owners:
        owners -= 1
    cw = nx // owners
    coef, zw, ey, ez = tables(ny, nz, ly, lz)
    toep, uw = x_tables()
    hbm = pl.BlockSpec(memory_space=pltpu.HBM)
    dma = pltpu.SemaphoreType.DMA
    f32 = jnp.float32
    out = pl.pallas_call(
        functools.partial(kernel, ny, nz, owners),
        out_shape=jax.ShapeDtypeStruct((rows, nx), f32),
        in_specs=[hbm] * 8,
        out_specs=hbm,
        scratch_shapes=[
            pltpu.VMEM((ly + 2, lz, nx + 2 * LANES), f32),
            pltpu.VMEM(speed.shape, speed.dtype),
            pltpu.VMEM((2, ly, nx), f32),
            pltpu.VMEM((2, ly, nx), f32),
            pltpu.VMEM((rows, nx), f32),
            pltpu.VMEM((nz * ly, nx), f32),
            pltpu.VMEM((2 * lz, nx), f32),
            pltpu.VMEM((total - corner, nx), f32),
            pltpu.VMEM((rows, nx), f32),
            pltpu.VMEM((rows, nx), f32),
            pltpu.VMEM((2 * lz, nx), f32),
            pltpu.VMEM((2, ly, nx), f32),
            pltpu.VMEM((ny, 2 * lz, cw), f32),
            pltpu.VMEM((ny, 2 * lz, cw), f32),
            pltpu.VMEM((2, 1, 2 * nx), f32),
            pltpu.VMEM((nz, 1, 2 * nx), f32),
            pltpu.SMEM(coef.shape, f32),
            pltpu.VMEM(zw.shape, f32),
            pltpu.VMEM((rows, total), f32),
            pltpu.VMEM((rows, total), f32),
            pltpu.VMEM(toep.shape, jnp.bfloat16),
            pltpu.VMEM(uw.shape, f32),
            dma((8,)), dma((nx // XB,)), dma((4, nx // 512)), dma((4, nx // 512)),
            dma((ny,)), dma((ny,)), dma((ny,)), dma((ny,)),
            dma((nz, nx // 512)), dma((nz, nx // 512)), dma((nz,)), dma((nz,)),
        ],
        compiler_params=pltpu.CompilerParams(collective_id=0, has_side_effects=True),
    )(heat, speed, jnp.asarray(coef), jnp.asarray(zw), jnp.asarray(ey), jnp.asarray(ez),
      jnp.asarray(toep), jnp.asarray(uw))
    return out.reshape(ly, lz, nx)


def solution(mesh):
    in_specs = (P("gy", "gz", None), P(None, "gy", "gz", None))
    return jax.shard_map(
        functools.partial(on_device, mesh.shape["gy"], mesh.shape["gz"]),
        mesh=mesh, in_specs=in_specs, out_specs=P("gy", "gz", None), check_vma=False,
    )
```

```python
import functools

import jax
import jax.numpy as jnp
import numpy as np
from jax import lax
from jax.experimental import pallas as pl
from jax.experimental.pallas import tpu as pltpu
from jax.sharding import PartitionSpec as P

RX = 1
RY = 768
RZ = 192
KAPPA = 0.15
XB = 256
LANES = 128
MESH = pl.DeviceIdType.MESH


def decay(ratio):
    h = 0.5 / ratio
    return 1.0 + h - np.sqrt(h * (2.0 + h))


def line_parts(n, ratio):
    q = decay(ratio)
    i = np.arange(n, dtype=np.float64)
    half = n / 2.0
    rise = q ** (-i + half) * (1.0 - q ** (2.0 * (i + 1.0)))
    fall = q ** (i + 1.0 - half) * (1.0 - q ** (2.0 * (n - i)))
    fall = fall / (ratio * (1.0 - q * q) * (1.0 - q ** (2.0 * n + 2.0)))
    return rise, fall


def line_block(rise, fall):
    n = len(rise)
    small = np.minimum(np.arange(n)[:, None], np.arange(n)[None, :])
    large = np.maximum(np.arange(n)[:, None], np.arange(n)[None, :])
    return rise[small] * fall[large]


def sizes(ny, nz, ly, lz):
    rows = ly * lz
    far_y = rows + nz * ly
    corner = far_y + 2 * lz
    total = corner + -(-2 * nz // 16) * 16
    return rows, far_y, corner, total


def tables(ny, nz, ly, lz):
    rows, far_y, corner, total = sizes(ny, nz, ly, lz)
    ry, fy = line_parts(ny * ly, RY)
    rz, fz = line_parts(nz * lz, RZ)
    ry, fy = ry.reshape(ny, ly), fy.reshape(ny, ly)
    rz, fz = rz.reshape(nz, lz), fz.reshape(nz, lz)
    ey = np.zeros((ny, ly, lz, total))
    ez = np.zeros((nz, ly, lz, total))
    for a in range(ny):
        block = line_block(ry[a], fy[a])
        ey[a, :, :, :rows] = np.repeat(block, lz, axis=1)[:, None, :]
        ey[a, :, :, rows:far_y] = np.tile(block, (1, nz))[:, None, :]
        ey[a, :, :, far_y : far_y + lz] = fy[a][:, None, None]
        ey[a, :, :, far_y + lz : corner] = ry[a][:, None, None]
        ey[a, :, :, corner : corner + 2 * nz : 2] = fy[a][:, None, None]
        ey[a, :, :, corner + 1 : corner + 2 * nz : 2] = ry[a][:, None, None]
    for c in range(nz):
        block = line_block(rz[c], fz[c])
        ez[c, :, :, :rows] = np.tile(block, (1, ly))[None]
        ez[c, :, :, far_y:corner] = np.tile(block, (1, 2))[None]
        for b in range(nz):
            weight = fz[c] if b < c else rz[c]
            if b != c:
                ez[c, :, :, rows + b * ly : rows + (b + 1) * ly] = weight[None, :, None]
                ez[c, :, :, corner + 2 * b : corner + 2 * b + 2] = weight[None, :, None]
    coef = np.concatenate([ry.reshape(-1), fy.reshape(-1)])
    zw = np.stack([rz, fz], axis=1)[..., None] * np.ones(LANES)
    f32 = lambda t: np.asarray(t, np.float32)
    return (
        f32(coef),
        f32(zw),
        f32(ey.reshape(ny, rows, total)),
        f32(ez.reshape(nz, rows, total)),
    )


def x_tables():
    q = decay(RX)
    i = np.arange(XB)
    toep = q ** np.abs(i[:, None] - i[None, :]) * q / (RX * (1.0 - q * q))
    toep = np.asarray(toep, np.float32)
    hi = toep.astype(jnp.bfloat16)
    lo = (toep - hi.astype(np.float32)).astype(jnp.bfloat16)
    uw = np.stack([q ** (i + 1.0), q ** (XB - i * 1.0)])[:, None, :] * np.ones((1, 8, 1))
    return np.stack([hi, lo]), np.asarray(uw, np.float32)


def split(x):
    hi = x.astype(jnp.bfloat16)
    return hi, (x - hi.astype(jnp.float32)).astype(jnp.bfloat16)


def dot(a, b):
    return jnp.dot(a, b, preferred_element_type=jnp.float32)


def dot3(a, b):
    return dot(a[0], b[0]) + (dot(a[1], b[0]) + dot(a[0], b[1]))


def dot_left(parts, x):
    hi, lo = split(x)
    return dot(parts, jnp.concatenate([hi, hi, lo], axis=0))


def left_parts(w):
    hi, lo = split(w)
    return jnp.concatenate([hi, lo, hi], axis=1)


def solve_x(pieces, toeplitz):
    blocks = len(pieces)
    rows = pieces[0].shape[0]
    hi, lo = split(jnp.concatenate(pieces, axis=0))
    local = dot(hi, toeplitz[0]) + (dot(lo, toeplitz[0]) + dot(hi, toeplitz[1]))
    return [local[a * rows : (a + 1) * rows] for a in range(blocks)]


def carries(heads, tails):
    blocks = len(heads)
    q = decay(RX)
    step = float(q**XB)
    nx = blocks * XB
    head, tail = heads[-1], tails[0]
    for a in range(1, blocks):
        tail = step * tail + tails[a]
        head = step * head + heads[blocks - 1 - a]
    scale = 1.0 / (1.0 - q ** (2.0 * nx + 2.0))
    near, far = float(-q * scale), float(q ** (nx + 2.0) * scale)
    ahead = [near * head + far * tail]
    after = [near * tail + far * head]
    for a in range(blocks - 1):
        ahead.append(step * ahead[-1] + tails[a])
        after.append(step * after[-1] + heads[blocks - 1 - a])
    return ahead, after[::-1]


def along_x(pieces, toeplitz, grow, fade):
    local = solve_x(pieces, toeplitz)
    ahead, after = carries([p[:, 0:1] for p in local], [p[:, XB - 1 : XB] for p in local])
    return [p + f * grow + g * fade for p, f, g in zip(local, ahead, after)]


def kernel(
    ny, nz, owners,
    heat, speed, coef_hbm, zw_hbm, ey_hbm, ez_hbm, toep_hbm, uw_hbm,
    partial, corners,
    field, vel, zsend, zhalo, data, far_z, far_y, corner_rows, mixed, acc,
    yface, zface, held, back, cface, chold, coef, zw, ey, ez, toep, uw,
    load_sem, out_sem, hs_send, hs_recv, a_send, a_recv, b_send, b_recv, z_send, z_recv, c_send, c_recv,
):
    ly, lz, nx = heat.shape
    rows, off_y, off_c, total = sizes(ny, nz, ly, lz)
    cw = nx // owners
    half = owners // 2
    blocks = nx // XB
    my = lax.axis_index("gy")
    mz = lax.axis_index("gz")
    inner = pl.ds(LANES, nx)

    loads = [
        pltpu.make_async_copy(heat, field.at[pl.ds(1, ly), :, inner], load_sem.at[0]),
        pltpu.make_async_copy(speed, vel, load_sem.at[1]),
        pltpu.make_async_copy(coef_hbm, coef, load_sem.at[2]),
        pltpu.make_async_copy(zw_hbm, zw, load_sem.at[3]),
        pltpu.make_async_copy(ey_hbm.at[my], ey, load_sem.at[4]),
        pltpu.make_async_copy(ez_hbm.at[mz], ez, load_sem.at[5]),
        pltpu.make_async_copy(toep_hbm, toep, load_sem.at[6]),
        pltpu.make_async_copy(uw_hbm, uw, load_sem.at[7]),
    ]
    loads[0].start()

    barrier = pltpu.get_barrier_semaphore()
    for d in range(1, ny):
        pl.semaphore_signal(barrier, 1, device_id={"gy": lax.rem(my + d, ny)}, device_id_type=MESH)
    for d in range(1, nz):
        pl.semaphore_signal(barrier, 1, device_id={"gz": lax.rem(mz + d, nz)}, device_id_type=MESH)
    for load in loads[1:]:
        load.start()

    first_y, last_y = my == 0, my == ny - 1
    first_z, last_z = mz == 0, mz == nz - 1
    edge = jnp.zeros((ly + 2, lz, LANES), jnp.float32)
    field[:, :, 0:LANES] = edge
    field[:, :, LANES + nx : 2 * LANES + nx] = edge

    @pl.when(first_y)
    def _():
        field[0, :, inner] = jnp.zeros((lz, nx), jnp.float32)

    @pl.when(last_y)
    def _():
        field[ly + 1, :, inner] = jnp.zeros((lz, nx), jnp.float32)

    @pl.when(first_z)
    def _():
        zhalo[0] = jnp.zeros((ly, nx), jnp.float32)

    @pl.when(last_z)
    def _():
        zhalo[1] = jnp.zeros((ly, nx), jnp.float32)

    far_z[pl.ds(pl.multiple_of(mz * ly, 8), ly), :] = jnp.zeros((ly, nx), jnp.float32)
    corner_rows[...] = jnp.zeros_like(corner_rows)
    chold[mz] = jnp.zeros((1, 2 * nx), jnp.float32)

    loads[0].wait()
    for y in range(ly):
        zsend[0, y : y + 1, :] = field[y + 1, 0:1, inner]
        zsend[1, y : y + 1, :] = field[y + 1, lz - 1 : lz, inner]
    pl.semaphore_wait(barrier, ny - 1 + nz - 1)

    def remote(src, dst, send, recv, target):
        return pltpu.make_async_remote_copy(
            src_ref=src, dst_ref=dst, send_sem=send, recv_sem=recv,
            device_id=target, device_id_type=MESH,
        )

    down_y = lax.rem(my + ny - 1, ny)
    up_y = lax.rem(my + 1, ny)
    down_z = lax.rem(mz + nz - 1, nz)
    up_z = lax.rem(mz + 1, nz)
    chunk = 512
    chunks = nx // chunk
    inside = (
        (jnp.logical_not(first_y), jnp.logical_not(last_y)),
        (jnp.logical_not(first_z), jnp.logical_not(last_z)),
    )
    ends = []
    for n in range(chunks):
        cols = pl.ds(n * chunk, chunk)
        mid = pl.ds(n * chunk + LANES, chunk)
        y_down = remote(
            field.at[1, :, mid], field.at[ly + 1, :, mid],
            hs_send.at[0, n], hs_recv.at[0, n], {"gy": down_y},
        )
        y_up = remote(
            field.at[ly, :, mid], field.at[0, :, mid],
            hs_send.at[1, n], hs_recv.at[1, n], {"gy": up_y},
        )
        z_down = remote(
            zsend.at[0, :, cols], zhalo.at[1, :, cols],
            hs_send.at[2, n], hs_recv.at[2, n], {"gz": down_z},
        )
        z_up = remote(
            zsend.at[1, :, cols], zhalo.at[0, :, cols],
            hs_send.at[3, n], hs_recv.at[3, n], {"gz": up_z},
        )
        ends.append((
            (inside[0][0], y_down, y_up), (inside[0][1], y_up, y_down),
            (inside[1][0], z_down, z_up), (inside[1][1], z_up, z_down),
        ))
    for end in ends:
        for there, sent, _ in end:
            pl.when(there)(lambda sent=sent: sent.start())

    for load in loads[1:]:
        load.wait()
    weights = ey[...] * ez[...]
    w_own = split(weights[:, :rows])
    w_z = left_parts(weights[:, rows:off_y])
    w_y = left_parts(weights[:, off_y:off_c])
    toeplitz = (toep[0], toep[1])
    grow, fade = uw[0, 0:1, :], uw[1, 0:1, :]

    def column(owner):
        if owners % 2 or owners == 1:
            return pl.multiple_of(owner * cw, LANES)
        block = jnp.where(owner < half, 2 * owner, 2 * (owners - 1 - owner) + 1)
        return pl.multiple_of(block * cw, LANES)

    def owner_of(block):
        if owners % 2 or owners == 1:
            return block
        return block // 2 if block % 2 == 0 else owners - 1 - block // 2

    def to_owner(owner):
        return remote(
            yface.at[:, pl.ds(column(owner), cw)], held.at[my],
            a_send.at[owner], a_recv.at[my], {"gy": owner},
        )

    def from_peer(peer):
        return remote(
            yface.at[:, pl.ds(0, cw)], held.at[peer], a_send.at[0], a_recv.at[peer], {"gy": peer}
        )

    def owned(index, body):
        if owners == ny:
            body()
        else:
            pl.when(index < owners)(body)

    tile = lambda w: jnp.concatenate([w] * (chunk // LANES), axis=1)
    rise_z = tile(zw[mz, 0])
    fall_z = tile(zw[mz, 1])
    level = lax.broadcasted_iota(jnp.int32, (lz, chunk), 0)
    wide = chunk + 2 * LANES

    z_copies = []
    for x in range(0, nx, chunk):
        for there, _, received in ends[x // chunk]:
            pl.when(there)(lambda received=received: received.wait_recv())
        cols = pl.ds(x, chunk)
        mid = pl.ds(x + LANES, chunk)

        def layer(y, sums, x=x, cols=cols, mid=mid):
            window = field[y + 1, :, pl.ds(x, wide)]
            here = window[:, LANES : LANES + chunk]
            east = pltpu.roll(window, wide - 1, 1)[:, LANES : LANES + chunk]
            west = pltpu.roll(window, 1, 1)[:, LANES : LANES + chunk]
            south, north = field[y, :, mid], field[y + 2, :, mid]
            row = pl.ds(y, 1)
            above = jnp.where(level == lz - 1, zhalo[1, row, cols], pltpu.roll(here, lz - 1, 0))
            below = jnp.where(level == 0, zhalo[0, row, cols], pltpu.roll(here, 1, 0))
            spread = (east + west) + (north + south) + (above + below)
            moved = (
                vel[0, y, :, cols].astype(jnp.float32) * (east - west)
                + vel[1, y, :, cols].astype(jnp.float32) * (north - south)
                + vel[2, y, :, cols].astype(jnp.float32) * (above - below)
            )
            source = (1.0 - 6.0 * KAPPA) * here + KAPPA * spread - 0.5 * moved
            data[pl.ds(pl.multiple_of(y * lz, lz), lz), cols] = source
            zface[0, row, cols] = jnp.sum(source * rise_z, axis=0, keepdims=True)
            zface[1, row, cols] = jnp.sum(source * fall_z, axis=0, keepdims=True)
            place = my * ly + y
            return (sums[0] + coef[place] * source, sums[1] + coef[ny * ly + place] * source)

        zero = jnp.zeros((lz, chunk), jnp.float32)
        rising, falling = lax.fori_loop(0, ly, layer, (zero, zero), unroll=4)
        yface[0:lz, cols] = rising
        yface[lz : 2 * lz, cols] = falling
        for block in range(x // cw, (x + chunk) // cw):
            owner = owner_of(block)
            pl.when(my != owner)(lambda owner=owner: to_owner(owner).start())

        for d in range(1, nz):
            peer = lax.rem(mz + d, nz)
            side = (mz + d) // nz
            slot = far_z.at[pl.ds(pl.multiple_of(mz * ly, 8), ly), cols]
            n = x // chunk
            copy = remote(
                zface.at[side, :, cols], slot, z_send.at[peer, n], z_recv.at[mz, n], {"gz": peer}
            )
            copy.start()
            z_copies.append(copy)

    parts = [slice(a * XB, (a + 1) * XB) for a in range(blocks)]
    for part in parts:
        mixed[:, part] = dot3(w_own, split(data[:, part]))

    def to_peer(peer):
        return remote(
            back.at[peer], far_y.at[:, pl.ds(column(my), cw)],
            b_send.at[peer], b_recv.at[my], {"gy": peer},
        )

    def from_owner(owner):
        return remote(
            back.at[0], far_y.at[:, pl.ds(column(owner), cw)],
            b_send.at[0], b_recv.at[owner], {"gy": owner},
        )

    def gather_sums():
        held[my] = yface[:, pl.ds(column(my), cw)]
        for d in range(1, ny):
            from_peer(lax.rem(my + d, ny)).wait_recv()
        run = jnp.zeros((lz, cw), jnp.float32)
        for a in range(ny):
            back[a, 0:lz, :] = run
            run = run + held[a, 0:lz, :]
        run = jnp.zeros((lz, cw), jnp.float32)
        for a in reversed(range(ny)):
            back[a, lz : 2 * lz, :] = run
            run = run + held[a, lz : 2 * lz, :]
        for d in range(1, ny):
            to_peer(lax.rem(my + d, ny)).start()
        far_y[:, pl.ds(column(my), cw)] = back[my]

    owned(my, gather_sums)

    for d in range(1, nz):
        peer = lax.rem(mz + d, nz)
        for n in range(chunks):
            cols = pl.ds(n * chunk, chunk)
            slot = far_z.at[pl.ds(pl.multiple_of(peer * ly, 8), ly), cols]
            remote(
                zface.at[0, :, cols], slot, z_send.at[0, n], z_recv.at[peer, n], {"gz": peer}
            ).wait_recv()
    both = [mixed[:, part] + dot_left(w_z, far_z[:, part]) for part in parts]
    for part, piece in zip(parts, along_x(both, toeplitz, grow, fade)):
        acc[:, part] = piece

    for d in range(1, ny):
        owner = lax.rem(my + d, ny)
        owned(owner, lambda owner=owner: from_owner(owner).wait_recv())

    whole = lambda w: jnp.concatenate([w] * (nx // LANES), axis=1)
    for side in range(2):
        weight = whole(zw[mz, side])
        for k in range(2):
            far = far_y[k * lz : (k + 1) * lz, :]
            cface[side, :, k * nx : (k + 1) * nx] = jnp.sum(far * weight, axis=0, keepdims=True)
    c_copies = []
    for d in range(1, nz):
        peer = lax.rem(mz + d, nz)
        side = (mz + d) // nz
        copy = remote(cface.at[side], chold.at[mz], c_send.at[peer], c_recv.at[mz], {"gz": peer})
        copy.start()
        c_copies.append(copy)

    solved = along_x([far_y[:, part] for part in parts], toeplitz, grow, fade)
    stores = []
    for a, (part, piece) in enumerate(zip(parts, solved)):
        acc[:, part] += dot_left(w_y, piece)
        place = pl.ds(a * XB, XB)
        stores.append(pltpu.make_async_copy(acc.at[:, place], partial.at[:, place], out_sem.at[a]))
        stores[-1].start()

    for d in range(1, nz):
        peer = lax.rem(mz + d, nz)
        remote(
            cface.at[0], chold.at[peer], c_send.at[0], c_recv.at[peer], {"gz": peer}
        ).wait_recv()
    for b in range(nz):
        for k in range(2):
            corner_rows[2 * b + k : 2 * b + k + 1, :] = chold[b, :, k * nx : (k + 1) * nx]
    stores.append(pltpu.make_async_copy(corner_rows, corners, out_sem.at[blocks]))
    stores[-1].start()

    for end in ends:
        for there, sent, _ in end:
            pl.when(there)(lambda sent=sent: sent.wait_send())
    for block in range(owners):
        owner = owner_of(block)
        pl.when(my != owner)(lambda owner=owner: to_owner(owner).wait_send())
    for copy in z_copies + c_copies:
        copy.wait_send()

    def sums_sent():
        for d in range(1, ny):
            to_peer(lax.rem(my + d, ny)).wait_send()

    owned(my, sums_sent)
    for store in stores:
        store.wait()


def finish(
    off_c, partial, corners, ey_hbm, ez_hbm, toep_hbm, uw_hbm, out,
    acc, rows_c, ey, ez, toep, uw, load_sem, in_sem, out_sem,
):
    blocks = partial.shape[1] // XB
    parts = [slice(a * XB, (a + 1) * XB) for a in range(blocks)]
    loads = [
        pltpu.make_async_copy(corners, rows_c, load_sem.at[0]),
        pltpu.make_async_copy(toep_hbm, toep, load_sem.at[1]),
        pltpu.make_async_copy(uw_hbm, uw, load_sem.at[2]),
        pltpu.make_async_copy(ey_hbm.at[lax.axis_index("gy")], ey, load_sem.at[3]),
        pltpu.make_async_copy(ez_hbm.at[lax.axis_index("gz")], ez, load_sem.at[4]),
    ]
    pieces_in, pieces_out = [], []
    for a in range(blocks):
        place = pl.ds(a * XB, XB)
        pieces_in.append(
            pltpu.make_async_copy(partial.at[:, place], acc.at[:, place], in_sem.at[a])
        )
        pieces_out.append(
            pltpu.make_async_copy(acc.at[:, place], out.at[:, place], out_sem.at[a])
        )
    for copy in loads + pieces_in:
        copy.start()
    for copy in loads:
        copy.wait()
    w_c = left_parts(ey[:, off_c:] * ez[:, off_c:])
    solved = along_x(
        [rows_c[:, part] for part in parts], (toep[0], toep[1]), uw[0, 0:1, :], uw[1, 0:1, :]
    )
    for a, part in enumerate(parts):
        far = dot_left(w_c, solved[a])
        pieces_in[a].wait()
        acc[:, part] += far
        pieces_out[a].start()
    for copy in pieces_out:
        copy.wait()


def on_device(ny, nz, heat, speed):
    ly, lz, nx = heat.shape
    rows, far_y, corner, total = sizes(ny, nz, ly, lz)
    owners = min(ny, nx // LANES)
    while (nx // LANES) % owners:
        owners -= 1
    cw = nx // owners
    coef, zw, ey, ez = tables(ny, nz, ly, lz)
    toep, uw = x_tables()
    hbm = pl.BlockSpec(memory_space=pltpu.HBM)
    dma = pltpu.SemaphoreType.DMA
    f32 = jnp.float32
    operands = [jnp.asarray(t) for t in (coef, zw, ey, ez, toep, uw)]
    partial, corners = pl.pallas_call(
        functools.partial(kernel, ny, nz, owners),
        out_shape=[
            jax.ShapeDtypeStruct((rows, nx), f32),
            jax.ShapeDtypeStruct((total - corner, nx), f32),
        ],
        in_specs=[hbm] * 8,
        out_specs=[hbm] * 2,
        scratch_shapes=[
            pltpu.VMEM((ly + 2, lz, nx + 2 * LANES), f32),
            pltpu.VMEM(speed.shape, speed.dtype),
            pltpu.VMEM((2, ly, nx), f32),
            pltpu.VMEM((2, ly, nx), f32),
            pltpu.VMEM((rows, nx), f32),
            pltpu.VMEM((nz * ly, nx), f32),
            pltpu.VMEM((2 * lz, nx), f32),
            pltpu.VMEM((total - corner, nx), f32),
            pltpu.VMEM((rows, nx), f32),
            pltpu.VMEM((rows, nx), f32),
            pltpu.VMEM((2 * lz, nx), f32),
            pltpu.VMEM((2, ly, nx), f32),
            pltpu.VMEM((ny, 2 * lz, cw), f32),
            pltpu.VMEM((ny, 2 * lz, cw), f32),
            pltpu.VMEM((2, 1, 2 * nx), f32),
            pltpu.VMEM((nz, 1, 2 * nx), f32),
            pltpu.SMEM(coef.shape, f32),
            pltpu.VMEM(zw.shape, f32),
            pltpu.VMEM((rows, total), f32),
            pltpu.VMEM((rows, total), f32),
            pltpu.VMEM(toep.shape, jnp.bfloat16),
            pltpu.VMEM(uw.shape, f32),
            dma((8,)), dma((nx // XB + 1,)), dma((4, nx // 512)), dma((4, nx // 512)),
            dma((ny,)), dma((ny,)), dma((ny,)), dma((ny,)),
            dma((nz, nx // 512)), dma((nz, nx // 512)), dma((nz,)), dma((nz,)),
        ],
        compiler_params=pltpu.CompilerParams(collective_id=0, has_side_effects=True),
    )(heat, speed, *operands)
    out = pl.pallas_call(
        functools.partial(finish, corner),
        out_shape=jax.ShapeDtypeStruct((rows, nx), f32),
        in_specs=[hbm] * 6,
        out_specs=hbm,
        scratch_shapes=[
            pltpu.VMEM((rows, nx), f32),
            pltpu.VMEM((total - corner, nx), f32),
            pltpu.VMEM((rows, total), f32),
            pltpu.VMEM((rows, total), f32),
            pltpu.VMEM(toep.shape, jnp.bfloat16),
            pltpu.VMEM(uw.shape, f32),
            dma((5,)), dma((nx // XB,)), dma((nx // XB,)),
        ],
    )(partial, corners, *operands[2:])
    return out.reshape(ly, lz, nx)


def solution(mesh):
    in_specs = (P("gy", "gz", None), P(None, "gy", "gz", None))
    return jax.shard_map(
        functools.partial(on_device, mesh.shape["gy"], mesh.shape["gz"]),
        mesh=mesh, in_specs=in_specs, out_specs=P("gy", "gz", None), check_vma=False,
    )
```

```python
import functools

import jax
import jax.numpy as jnp
import numpy as np
from jax import lax
from jax.experimental import pallas as pl
from jax.experimental.pallas import tpu as pltpu
from jax.sharding import PartitionSpec as P

RX = 1
RY = 768
RZ = 192
KAPPA = 0.15
XB = 256
LANES = 128
MESH = pl.DeviceIdType.MESH


def decay(ratio):
    h = 0.5 / ratio
    return 1.0 + h - np.sqrt(h * (2.0 + h))


def line_parts(n, ratio):
    q = decay(ratio)
    i = np.arange(n, dtype=np.float64)
    half = n / 2.0
    rise = q ** (-i + half) * (1.0 - q ** (2.0 * (i + 1.0)))
    fall = q ** (i + 1.0 - half) * (1.0 - q ** (2.0 * (n - i)))
    fall = fall / (ratio * (1.0 - q * q) * (1.0 - q ** (2.0 * n + 2.0)))
    return rise, fall


def line_block(rise, fall):
    n = len(rise)
    small = np.minimum(np.arange(n)[:, None], np.arange(n)[None, :])
    large = np.maximum(np.arange(n)[:, None], np.arange(n)[None, :])
    return rise[small] * fall[large]


def sizes(ny, nz, ly, lz):
    rows = ly * lz
    far_y = rows + nz * ly
    corner = far_y + 2 * lz
    total = corner + -(-2 * nz // 16) * 16
    return rows, far_y, corner, total


def tables(ny, nz, ly, lz):
    rows, far_y, corner, total = sizes(ny, nz, ly, lz)
    ry, fy = line_parts(ny * ly, RY)
    rz, fz = line_parts(nz * lz, RZ)
    ry, fy = ry.reshape(ny, ly), fy.reshape(ny, ly)
    rz, fz = rz.reshape(nz, lz), fz.reshape(nz, lz)
    ey = np.zeros((ny, ly, lz, total))
    ez = np.zeros((nz, ly, lz, total))
    for a in range(ny):
        block = line_block(ry[a], fy[a])
        ey[a, :, :, :rows] = np.repeat(block, lz, axis=1)[:, None, :]
        ey[a, :, :, rows:far_y] = np.tile(block, (1, nz))[:, None, :]
        ey[a, :, :, far_y : far_y + lz] = fy[a][:, None, None]
        ey[a, :, :, far_y + lz : corner] = ry[a][:, None, None]
        ey[a, :, :, corner : corner + 2 * nz : 2] = fy[a][:, None, None]
        ey[a, :, :, corner + 1 : corner + 2 * nz : 2] = ry[a][:, None, None]
    for c in range(nz):
        block = line_block(rz[c], fz[c])
        ez[c, :, :, :rows] = np.tile(block, (1, ly))[None]
        ez[c, :, :, far_y:corner] = np.tile(block, (1, 2))[None]
        for b in range(nz):
            weight = fz[c] if b < c else rz[c]
            if b != c:
                ez[c, :, :, rows + b * ly : rows + (b + 1) * ly] = weight[None, :, None]
                ez[c, :, :, corner + 2 * b : corner + 2 * b + 2] = weight[None, :, None]
    coef = np.concatenate([ry.reshape(-1), fy.reshape(-1)])
    zw = np.stack([rz, fz], axis=1)[..., None] * np.ones(LANES)
    f32 = lambda t: np.asarray(t, np.float32)
    return (
        f32(coef),
        f32(zw),
        f32(ey.reshape(ny, rows, total)),
        f32(ez.reshape(nz, rows, total)),
    )


def x_tables():
    q = decay(RX)
    i = np.arange(XB)
    toep = q ** np.abs(i[:, None] - i[None, :]) * q / (RX * (1.0 - q * q))
    toep = np.asarray(toep, np.float32)
    hi = toep.astype(jnp.bfloat16)
    lo = (toep - hi.astype(np.float32)).astype(jnp.bfloat16)
    uw = np.stack([q ** (i + 1.0), q ** (XB - i * 1.0)])[:, None, :] * np.ones((1, 8, 1))
    return np.stack([hi, lo]), np.asarray(uw, np.float32)


def split(x):
    hi = x.astype(jnp.bfloat16)
    return hi, (x - hi.astype(jnp.float32)).astype(jnp.bfloat16)


def dot(a, b):
    return jnp.dot(a, b, preferred_element_type=jnp.float32)


def dot3(a, b):
    return dot(a[0], b[0]) + (dot(a[1], b[0]) + dot(a[0], b[1]))


def dot_left(parts, x):
    hi, lo = split(x)
    return dot(parts, jnp.concatenate([hi, hi, lo], axis=0))


def left_parts(w):
    hi, lo = split(w)
    return jnp.concatenate([hi, lo, hi], axis=1)


def solve_x(pieces, toeplitz):
    blocks = len(pieces)
    rows = pieces[0].shape[0]
    hi, lo = split(jnp.concatenate(pieces, axis=0))
    local = dot(hi, toeplitz[0]) + (dot(lo, toeplitz[0]) + dot(hi, toeplitz[1]))
    return [local[a * rows : (a + 1) * rows] for a in range(blocks)]


def carries(heads, tails):
    blocks = len(heads)
    q = decay(RX)
    step = float(q**XB)
    nx = blocks * XB
    head, tail = heads[-1], tails[0]
    for a in range(1, blocks):
        tail = step * tail + tails[a]
        head = step * head + heads[blocks - 1 - a]
    scale = 1.0 / (1.0 - q ** (2.0 * nx + 2.0))
    near, far = float(-q * scale), float(q ** (nx + 2.0) * scale)
    ahead = [near * head + far * tail]
    after = [near * tail + far * head]
    for a in range(blocks - 1):
        ahead.append(step * ahead[-1] + tails[a])
        after.append(step * after[-1] + heads[blocks - 1 - a])
    return ahead, after[::-1]


def along_x(pieces, toeplitz, grow, fade):
    local = solve_x(pieces, toeplitz)
    ahead, after = carries([p[:, 0:1] for p in local], [p[:, XB - 1 : XB] for p in local])
    return [p + f * grow + g * fade for p, f, g in zip(local, ahead, after)]


def kernel(
    ny, nz, owners,
    heat, speed, table,
    out,
    field, vel, zsend, zhalo, data, far_z, far_y, corner_rows, mixed, acc,
    yface, zface, held, back, cface, chold, coef, zw, ey, ez, toep, uw,
    load_sem, out_sem, hs_send, hs_recv, a_send, a_recv, b_send, b_recv, z_send, z_recv, c_send, c_recv,
):
    ly, lz, nx = heat.shape
    rows, off_y, off_c, total = sizes(ny, nz, ly, lz)
    cw = nx // owners
    half = owners // 2
    blocks = nx // XB
    my = lax.axis_index("gy")
    mz = lax.axis_index("gz")
    inner = pl.ds(LANES, nx)

    loads = [
        pltpu.make_async_copy(heat, field.at[pl.ds(1, ly), :, inner], load_sem.at[0]),
        pltpu.make_async_copy(speed, vel, load_sem.at[1]),
        pltpu.make_async_copy(
            table.at[ny + nz + 6 + my // 4, pl.ds(pl.multiple_of(my % 4 * 32, 32), 16)],
            coef.at[0], load_sem.at[2],
        ),
        pltpu.make_async_copy(
            table.at[ny + nz + 6 + my // 4, pl.ds(pl.multiple_of(my % 4 * 32 + 16, 16), 16)],
            coef.at[1], load_sem.at[8],
        ),
        pltpu.make_async_copy(
            table.at[ny + nz + 4, pl.ds(pl.multiple_of(mz * 16, 16), 16)], zw, load_sem.at[3]
        ),
        pltpu.make_async_copy(table.at[my], ey, load_sem.at[4]),
        pltpu.make_async_copy(table.at[ny + mz], ez, load_sem.at[5]),
        pltpu.make_async_copy(table.at[pl.ds(ny + nz, 4)], toep, load_sem.at[6]),
        pltpu.make_async_copy(table.at[ny + nz + 5, pl.ds(0, 16)], uw, load_sem.at[7]),
    ]
    loads[0].start()

    barrier = pltpu.get_barrier_semaphore()
    for d in range(1, ny):
        pl.semaphore_signal(barrier, 1, device_id={"gy": lax.rem(my + d, ny)}, device_id_type=MESH)
    for d in range(1, nz):
        pl.semaphore_signal(barrier, 1, device_id={"gz": lax.rem(mz + d, nz)}, device_id_type=MESH)
    for load in loads[1:]:
        load.start()

    first_y, last_y = my == 0, my == ny - 1
    first_z, last_z = mz == 0, mz == nz - 1
    edge = jnp.zeros((ly + 2, lz, LANES), jnp.float32)
    field[:, :, 0:LANES] = edge
    field[:, :, LANES + nx : 2 * LANES + nx] = edge

    @pl.when(first_y)
    def _():
        field[0, :, inner] = jnp.zeros((lz, nx), jnp.float32)

    @pl.when(last_y)
    def _():
        field[ly + 1, :, inner] = jnp.zeros((lz, nx), jnp.float32)

    @pl.when(first_z)
    def _():
        zhalo[0] = jnp.zeros((ly, nx), jnp.float32)

    @pl.when(last_z)
    def _():
        zhalo[1] = jnp.zeros((ly, nx), jnp.float32)

    far_z[pl.ds(pl.multiple_of(mz * ly, 8), ly), :] = jnp.zeros((ly, nx), jnp.float32)
    corner_rows[...] = jnp.zeros_like(corner_rows)
    chold[mz] = jnp.zeros((1, 2 * nx), jnp.float32)

    loads[0].wait()
    for y in range(ly):
        zsend[0, y : y + 1, :] = field[y + 1, 0:1, inner]
        zsend[1, y : y + 1, :] = field[y + 1, lz - 1 : lz, inner]
    pl.semaphore_wait(barrier, ny - 1 + nz - 1)

    def remote(src, dst, send, recv, target):
        return pltpu.make_async_remote_copy(
            src_ref=src, dst_ref=dst, send_sem=send, recv_sem=recv,
            device_id=target, device_id_type=MESH,
        )

    down_y = lax.rem(my + ny - 1, ny)
    up_y = lax.rem(my + 1, ny)
    down_z = lax.rem(mz + nz - 1, nz)
    up_z = lax.rem(mz + 1, nz)
    chunk = 512
    chunks = nx // chunk
    inside = (
        (jnp.logical_not(first_y), jnp.logical_not(last_y)),
        (jnp.logical_not(first_z), jnp.logical_not(last_z)),
    )
    ends = []
    for n in range(chunks):
        cols = pl.ds(n * chunk, chunk)
        mid = pl.ds(n * chunk + LANES, chunk)
        y_down = remote(
            field.at[1, :, mid], field.at[ly + 1, :, mid],
            hs_send.at[0, n], hs_recv.at[0, n], {"gy": down_y},
        )
        y_up = remote(
            field.at[ly, :, mid], field.at[0, :, mid],
            hs_send.at[1, n], hs_recv.at[1, n], {"gy": up_y},
        )
        z_down = remote(
            zsend.at[0, :, cols], zhalo.at[1, :, cols],
            hs_send.at[2, n], hs_recv.at[2, n], {"gz": down_z},
        )
        z_up = remote(
            zsend.at[1, :, cols], zhalo.at[0, :, cols],
            hs_send.at[3, n], hs_recv.at[3, n], {"gz": up_z},
        )
        ends.append((
            (inside[0][0], y_down, y_up), (inside[0][1], y_up, y_down),
            (inside[1][0], z_down, z_up), (inside[1][1], z_up, z_down),
        ))
    for end in ends:
        for there, sent, _ in end:
            pl.when(there)(lambda sent=sent: sent.start())

    for load in loads[1:]:
        load.wait()
    weights = ey[...] * ez[...]
    w_own = split(weights[:, :rows])
    w_z = left_parts(weights[:, rows:off_y])
    w_y = left_parts(weights[:, off_y:off_c])
    w_c = left_parts(weights[:, off_c:total])
    toeplitz = tuple(
        jnp.concatenate([toep[2 * k, :, 0:XB], toep[2 * k + 1, :, 0:XB]], axis=0).astype(jnp.bfloat16)
        for k in range(2)
    )
    grow, fade = uw[0:1, 0:XB], uw[8:9, 0:XB]

    def column(owner):
        if owners % 2 or owners == 1:
            return pl.multiple_of(owner * cw, LANES)
        block = jnp.where(owner < half, 2 * owner, 2 * (owners - 1 - owner) + 1)
        return pl.multiple_of(block * cw, LANES)

    def owner_of(block):
        if owners % 2 or owners == 1:
            return block
        return block // 2 if block % 2 == 0 else owners - 1 - block // 2

    def to_owner(owner):
        return remote(
            yface.at[:, pl.ds(column(owner), cw)], held.at[my],
            a_send.at[owner], a_recv.at[my], {"gy": owner},
        )

    def from_peer(peer):
        return remote(
            yface.at[:, pl.ds(0, cw)], held.at[peer], a_send.at[0], a_recv.at[peer], {"gy": peer}
        )

    def owned(index, body):
        if owners == ny:
            body()
        else:
            pl.when(index < owners)(body)

    tile = lambda w: jnp.concatenate([w] * (chunk // LANES), axis=1)
    rise_z = tile(zw[0:8, 0:LANES])
    fall_z = tile(zw[8:16, 0:LANES])
    level = lax.broadcasted_iota(jnp.int32, (lz, chunk), 0)
    wide = chunk + 2 * LANES

    z_copies = []
    for x in range(0, nx, chunk):
        for there, _, received in ends[x // chunk]:
            pl.when(there)(lambda received=received: received.wait_recv())
        cols = pl.ds(x, chunk)
        mid = pl.ds(x + LANES, chunk)

        def layer(y, sums, x=x, cols=cols, mid=mid):
            window = field[y + 1, :, pl.ds(x, wide)]
            here = window[:, LANES : LANES + chunk]
            east = pltpu.roll(window, wide - 1, 1)[:, LANES : LANES + chunk]
            west = pltpu.roll(window, 1, 1)[:, LANES : LANES + chunk]
            south, north = field[y, :, mid], field[y + 2, :, mid]
            row = pl.ds(y, 1)
            above = jnp.where(level == lz - 1, zhalo[1, row, cols], pltpu.roll(here, lz - 1, 0))
            below = jnp.where(level == 0, zhalo[0, row, cols], pltpu.roll(here, 1, 0))
            spread = (east + west) + (north + south) + (above + below)
            moved = (
                vel[0, y, :, cols].astype(jnp.float32) * (east - west)
                + vel[1, y, :, cols].astype(jnp.float32) * (north - south)
                + vel[2, y, :, cols].astype(jnp.float32) * (above - below)
            )
            source = (1.0 - 6.0 * KAPPA) * here + KAPPA * spread - 0.5 * moved
            data[pl.ds(pl.multiple_of(y * lz, lz), lz), cols] = source
            zface[0, row, cols] = jnp.sum(source * rise_z, axis=0, keepdims=True)
            zface[1, row, cols] = jnp.sum(source * fall_z, axis=0, keepdims=True)
            rise_y = jnp.concatenate([coef[0, pl.ds(y, 1), 0:XB]] * (chunk // XB), axis=1)
            fall_y = jnp.concatenate([coef[1, pl.ds(y, 1), 0:XB]] * (chunk // XB), axis=1)
            return (sums[0] + rise_y * source, sums[1] + fall_y * source)

        zero = jnp.zeros((lz, chunk), jnp.float32)
        rising, falling = lax.fori_loop(0, ly, layer, (zero, zero), unroll=4)
        yface[0:lz, cols] = rising
        yface[lz : 2 * lz, cols] = falling
        for block in range(x // cw, (x + chunk) // cw):
            owner = owner_of(block)
            pl.when(my != owner)(lambda owner=owner: to_owner(owner).start())

        for d in range(1, nz):
            peer = lax.rem(mz + d, nz)
            side = (mz + d) // nz
            slot = far_z.at[pl.ds(pl.multiple_of(mz * ly, 8), ly), cols]
            n = x // chunk
            copy = remote(
                zface.at[side, :, cols], slot, z_send.at[peer, n], z_recv.at[mz, n], {"gz": peer}
            )
            copy.start()
            z_copies.append(copy)

    parts = [slice(a * XB, (a + 1) * XB) for a in range(blocks)]
    for part in parts:
        mixed[:, part] = dot3(w_own, split(data[:, part]))

    def to_peer(peer):
        return remote(
            back.at[peer], far_y.at[:, pl.ds(column(my), cw)],
            b_send.at[peer], b_recv.at[my], {"gy": peer},
        )

    def from_owner(owner):
        return remote(
            back.at[0], far_y.at[:, pl.ds(column(owner), cw)],
            b_send.at[0], b_recv.at[owner], {"gy": owner},
        )

    def gather_sums():
        held[my] = yface[:, pl.ds(column(my), cw)]
        for d in range(1, ny):
            from_peer(lax.rem(my + d, ny)).wait_recv()
        run = jnp.zeros((lz, cw), jnp.float32)
        for a in range(ny):
            back[a, 0:lz, :] = run
            run = run + held[a, 0:lz, :]
        run = jnp.zeros((lz, cw), jnp.float32)
        for a in reversed(range(ny)):
            back[a, lz : 2 * lz, :] = run
            run = run + held[a, lz : 2 * lz, :]
        for d in range(1, ny):
            to_peer(lax.rem(my + d, ny)).start()
        far_y[:, pl.ds(column(my), cw)] = back[my]

    owned(my, gather_sums)

    for d in range(1, nz):
        peer = lax.rem(mz + d, nz)
        for n in range(chunks):
            cols = pl.ds(n * chunk, chunk)
            slot = far_z.at[pl.ds(pl.multiple_of(peer * ly, 8), ly), cols]
            remote(
                zface.at[0, :, cols], slot, z_send.at[0, n], z_recv.at[peer, n], {"gz": peer}
            ).wait_recv()
    both = [mixed[:, part] + dot_left(w_z, far_z[:, part]) for part in parts]
    for part, piece in zip(parts, along_x(both, toeplitz, grow, fade)):
        acc[:, part] = piece

    for d in range(1, ny):
        owner = lax.rem(my + d, ny)
        owned(owner, lambda owner=owner: from_owner(owner).wait_recv())

    whole = lambda w: jnp.concatenate([w] * (nx // LANES), axis=1)
    for side in range(2):
        weight = whole(zw[8 * side : 8 * side + 8, 0:LANES])
        for k in range(2):
            far = far_y[k * lz : (k + 1) * lz, :]
            cface[side, :, k * nx : (k + 1) * nx] = jnp.sum(far * weight, axis=0, keepdims=True)
    c_copies = []
    for d in range(1, nz):
        peer = lax.rem(mz + d, nz)
        side = (mz + d) // nz
        copy = remote(cface.at[side], chold.at[mz], c_send.at[peer], c_recv.at[mz], {"gz": peer})
        copy.start()
        c_copies.append(copy)

    solved = along_x([far_y[:, part] for part in parts], toeplitz, grow, fade)
    for part, piece in zip(parts, solved):
        acc[:, part] += dot_left(w_y, piece)

    for d in range(1, nz):
        peer = lax.rem(mz + d, nz)
        remote(
            cface.at[0], chold.at[peer], c_send.at[0], c_recv.at[peer], {"gz": peer}
        ).wait_recv()
    for b in range(nz):
        for k in range(2):
            corner_rows[2 * b + k : 2 * b + k + 1, :] = chold[b, :, k * nx : (k + 1) * nx]
    solved = along_x([corner_rows[:, part] for part in parts], toeplitz, grow, fade)
    stores = []
    for a, (part, piece) in enumerate(zip(parts, solved)):
        acc[:, part] += dot_left(w_c, piece)
        place = pl.ds(a * XB, XB)
        stores.append(pltpu.make_async_copy(acc.at[:, place], out.at[:, place], out_sem.at[a]))
        stores[-1].start()

    for end in ends:
        for there, sent, _ in end:
            pl.when(there)(lambda sent=sent: sent.wait_send())
    for block in range(owners):
        owner = owner_of(block)
        pl.when(my != owner)(lambda owner=owner: to_owner(owner).wait_send())
    for copy in z_copies + c_copies:
        copy.wait_send()

    def sums_sent():
        for d in range(1, ny):
            to_peer(lax.rem(my + d, ny)).wait_send()

    owned(my, sums_sent)
    for store in stores:
        store.wait()


def on_device(ny, nz, heat, speed):
    ly, lz, nx = heat.shape
    rows, far_y, corner, total = sizes(ny, nz, ly, lz)
    owners = min(ny, nx // LANES)
    while (nx // LANES) % owners:
        owners -= 1
    cw = nx // owners
    coef, zw, ey, ez = tables(ny, nz, ly, lz)
    toep, uw = x_tables()
    wide = -(-total // XB) * XB
    table = np.zeros((ny + nz + 6 + -(-ny // 4), rows, wide), np.float32)
    table[:ny, :, :total] = ey
    table[ny : ny + nz, :, :total] = ez
    table[ny + nz : ny + nz + 4, :, :XB] = toep.astype(np.float32).reshape(4, rows, XB)
    table[ny + nz + 4, : 16 * nz, :LANES] = zw.reshape(16 * nz, LANES)
    table[ny + nz + 5, :16, :XB] = uw.reshape(16, XB)
    for a in range(ny):
        slab, row = ny + nz + 6 + a // 4, a % 4 * 32
        table[slab, row : row + 32] = coef.reshape(2, ny, ly)[:, a].reshape(32, 1)
    hbm = pl.BlockSpec(memory_space=pltpu.HBM)
    dma = pltpu.SemaphoreType.DMA
    f32 = jnp.float32
    out = pl.pallas_call(
        functools.partial(kernel, ny, nz, owners),
        out_shape=jax.ShapeDtypeStruct((rows, nx), f32),
        in_specs=[hbm] * 3,
        out_specs=hbm,
        scratch_shapes=[
            pltpu.VMEM((ly + 2, lz, nx + 2 * LANES), f32),
            pltpu.VMEM(speed.shape, speed.dtype),
            pltpu.VMEM((2, ly, nx), f32),
            pltpu.VMEM((2, ly, nx), f32),
            pltpu.VMEM((rows, nx), f32),
            pltpu.VMEM((nz * ly, nx), f32),
            pltpu.VMEM((2 * lz, nx), f32),
            pltpu.VMEM((total - corner, nx), f32),
            pltpu.VMEM((rows, nx), f32),
            pltpu.VMEM((rows, nx), f32),
            pltpu.VMEM((2 * lz, nx), f32),
            pltpu.VMEM((2, ly, nx), f32),
            pltpu.VMEM((ny, 2 * lz, cw), f32),
            pltpu.VMEM((ny, 2 * lz, cw), f32),
            pltpu.VMEM((2, 1, 2 * nx), f32),
            pltpu.VMEM((nz, 1, 2 * nx), f32),
            pltpu.VMEM((2, 16, wide), f32),
            pltpu.VMEM((16, wide), f32),
            pltpu.VMEM((rows, wide), f32),
            pltpu.VMEM((rows, wide), f32),
            pltpu.VMEM((4, rows, wide), f32),
            pltpu.VMEM((16, wide), f32),
            dma((9,)), dma((nx // XB,)), dma((4, nx // 512)), dma((4, nx // 512)),
            dma((ny,)), dma((ny,)), dma((ny,)), dma((ny,)),
            dma((nz, nx // 512)), dma((nz, nx // 512)), dma((nz,)), dma((nz,)),
        ],
        compiler_params=pltpu.CompilerParams(collective_id=0, has_side_effects=True, vmem_limit_bytes=53336 * 1024),
    )(heat, speed, jnp.asarray(table))
    return out.reshape(ly, lz, nx)


def solution(mesh):
    in_specs = (P("gy", "gz", None), P(None, "gy", "gz", None))
    return jax.shard_map(
        functools.partial(on_device, mesh.shape["gy"], mesh.shape["gz"]),
        mesh=mesh, in_specs=in_specs, out_specs=P("gy", "gz", None), check_vma=False,
    )
```

```python
import functools

import jax
import jax.numpy as jnp
import numpy as np
from jax import lax
from jax.experimental import pallas as pl
from jax.experimental.pallas import tpu as pltpu
from jax.sharding import PartitionSpec as P

RX = 1
RY = 768
RZ = 192
KAPPA = 0.15
XB = 256
LANES = 128
MESH = pl.DeviceIdType.MESH


def decay(ratio):
    h = 0.5 / ratio
    return 1.0 + h - np.sqrt(h * (2.0 + h))


def line_parts(n, ratio):
    q = decay(ratio)
    i = np.arange(n, dtype=np.float64)
    half = n / 2.0
    rise = q ** (-i + half) * (1.0 - q ** (2.0 * (i + 1.0)))
    fall = q ** (i + 1.0 - half) * (1.0 - q ** (2.0 * (n - i)))
    fall = fall / (ratio * (1.0 - q * q) * (1.0 - q ** (2.0 * n + 2.0)))
    return rise, fall


def line_block(rise, fall):
    n = len(rise)
    small = np.minimum(np.arange(n)[:, None], np.arange(n)[None, :])
    large = np.maximum(np.arange(n)[:, None], np.arange(n)[None, :])
    return rise[small] * fall[large]


def sizes(ny, nz, ly, lz):
    rows = ly * lz
    far_y = rows + nz * ly
    corner = far_y + 2 * lz
    total = corner + -(-2 * nz // 16) * 16
    return rows, far_y, corner, total


def tables(ny, nz, ly, lz):
    rows, far_y, corner, total = sizes(ny, nz, ly, lz)
    ry, fy = line_parts(ny * ly, RY)
    rz, fz = line_parts(nz * lz, RZ)
    ry, fy = ry.reshape(ny, ly), fy.reshape(ny, ly)
    rz, fz = rz.reshape(nz, lz), fz.reshape(nz, lz)
    ey = np.zeros((ny, ly, lz, total))
    ez = np.zeros((nz, ly, lz, total))
    for a in range(ny):
        block = line_block(ry[a], fy[a])
        ey[a, :, :, :rows] = np.repeat(block, lz, axis=1)[:, None, :]
        ey[a, :, :, rows:far_y] = np.tile(block, (1, nz))[:, None, :]
        ey[a, :, :, far_y : far_y + lz] = fy[a][:, None, None]
        ey[a, :, :, far_y + lz : corner] = ry[a][:, None, None]
        ey[a, :, :, corner : corner + 2 * nz : 2] = fy[a][:, None, None]
        ey[a, :, :, corner + 1 : corner + 2 * nz : 2] = ry[a][:, None, None]
    for c in range(nz):
        block = line_block(rz[c], fz[c])
        ez[c, :, :, :rows] = np.tile(block, (1, ly))[None]
        ez[c, :, :, far_y:corner] = np.tile(block, (1, 2))[None]
        for b in range(nz):
            weight = fz[c] if b < c else rz[c]
            if b != c:
                ez[c, :, :, rows + b * ly : rows + (b + 1) * ly] = weight[None, :, None]
                ez[c, :, :, corner + 2 * b : corner + 2 * b + 2] = weight[None, :, None]
    coef = np.concatenate([ry.reshape(-1), fy.reshape(-1)])
    zw = np.stack([rz, fz], axis=1)[..., None] * np.ones(LANES)
    f32 = lambda t: np.asarray(t, np.float32)
    return (
        f32(coef),
        f32(zw),
        f32(ey.reshape(ny, rows, total)),
        f32(ez.reshape(nz, rows, total)),
    )


def x_tables():
    q = decay(RX)
    i = np.arange(XB)
    toep = q ** np.abs(i[:, None] - i[None, :]) * q / (RX * (1.0 - q * q))
    toep = np.asarray(toep, np.float32)
    hi = toep.astype(jnp.bfloat16)
    lo = (toep - hi.astype(np.float32)).astype(jnp.bfloat16)
    uw = np.stack([q ** (i + 1.0), q ** (XB - i * 1.0)])[:, None, :] * np.ones((1, 8, 1))
    return np.stack([hi, lo]), np.asarray(uw, np.float32)


def split(x):
    hi = x.astype(jnp.bfloat16)
    return hi, (x - hi.astype(jnp.float32)).astype(jnp.bfloat16)


def dot(a, b):
    return jnp.dot(a, b, preferred_element_type=jnp.float32)


def dot3(a, b):
    return dot(a[0], b[0]) + (dot(a[1], b[0]) + dot(a[0], b[1]))


def dot_left(parts, x):
    hi, lo = split(x)
    return dot(parts, jnp.concatenate([hi, hi, lo], axis=0))


def left_parts(w):
    hi, lo = split(w)
    return jnp.concatenate([hi, lo, hi], axis=1)


def solve_x(pieces, toeplitz):
    blocks = len(pieces)
    rows = pieces[0].shape[0]
    hi, lo = split(jnp.concatenate(pieces, axis=0))
    local = dot(hi, toeplitz[0]) + (dot(lo, toeplitz[0]) + dot(hi, toeplitz[1]))
    return [local[a * rows : (a + 1) * rows] for a in range(blocks)]


def carries(heads, tails):
    blocks = len(heads)
    q = decay(RX)
    step = float(q**XB)
    nx = blocks * XB
    head, tail = heads[-1], tails[0]
    for a in range(1, blocks):
        tail = step * tail + tails[a]
        head = step * head + heads[blocks - 1 - a]
    scale = 1.0 / (1.0 - q ** (2.0 * nx + 2.0))
    near, far = float(-q * scale), float(q ** (nx + 2.0) * scale)
    ahead = [near * head + far * tail]
    after = [near * tail + far * head]
    for a in range(blocks - 1):
        ahead.append(step * ahead[-1] + tails[a])
        after.append(step * after[-1] + heads[blocks - 1 - a])
    return ahead, after[::-1]


def along_x(pieces, toeplitz, grow, fade):
    local = solve_x(pieces, toeplitz)
    ahead, after = carries([p[:, 0:1] for p in local], [p[:, XB - 1 : XB] for p in local])
    return [p + f * grow + g * fade for p, f, g in zip(local, ahead, after)]


def kernel(
    ny, nz, owners,
    heat, speed, table,
    out,
    field, vel, zsend, zhalo, data, far_z, far_y, corner_rows, mixed, acc,
    yface, zface, held, back, cface, chold, coef, zw, ey, ez, toep, uw,
    load_sem, out_sem, hs_send, hs_recv, a_send, a_recv, b_send, b_recv, z_send, z_recv, c_send, c_recv,
):
    ly, lz, nx = heat.shape
    rows, off_y, off_c, total = sizes(ny, nz, ly, lz)
    cw = nx // owners
    half = owners // 2
    blocks = nx // XB
    my = lax.axis_index("gy")
    mz = lax.axis_index("gz")
    inner = pl.ds(LANES, nx)

    loads = [
        pltpu.make_async_copy(heat, field.at[pl.ds(1, ly), :, inner], load_sem.at[0]),
        pltpu.make_async_copy(speed, vel, load_sem.at[1]),
        pltpu.make_async_copy(
            table.at[ny + nz + 6 + my // 4, pl.ds(pl.multiple_of(my % 4 * 32, 32), 16)],
            coef.at[0], load_sem.at[2],
        ),
        pltpu.make_async_copy(
            table.at[ny + nz + 6 + my // 4, pl.ds(pl.multiple_of(my % 4 * 32 + 16, 16), 16)],
            coef.at[1], load_sem.at[8],
        ),
        pltpu.make_async_copy(
            table.at[ny + nz + 4, pl.ds(pl.multiple_of(mz * 16, 16), 16)], zw, load_sem.at[3]
        ),
        pltpu.make_async_copy(table.at[my], ey, load_sem.at[4]),
        pltpu.make_async_copy(table.at[ny + mz], ez, load_sem.at[5]),
        pltpu.make_async_copy(table.at[pl.ds(ny + nz, 4)], toep, load_sem.at[6]),
        pltpu.make_async_copy(table.at[ny + nz + 5, pl.ds(0, 16)], uw, load_sem.at[7]),
    ]
    loads[0].start()

    barrier = pltpu.get_barrier_semaphore()
    for d in range(1, ny):
        pl.semaphore_signal(barrier, 1, device_id={"gy": lax.rem(my + d, ny)}, device_id_type=MESH)
    for d in range(1, nz):
        pl.semaphore_signal(barrier, 1, device_id={"gz": lax.rem(mz + d, nz)}, device_id_type=MESH)
    for load in loads[1:]:
        load.start()

    first_y, last_y = my == 0, my == ny - 1
    first_z, last_z = mz == 0, mz == nz - 1
    edge = jnp.zeros((ly + 2, lz, LANES), jnp.float32)
    field[:, :, 0:LANES] = edge
    field[:, :, LANES + nx : 2 * LANES + nx] = edge

    @pl.when(first_y)
    def _():
        field[0, :, inner] = jnp.zeros((lz, nx), jnp.float32)

    @pl.when(last_y)
    def _():
        field[ly + 1, :, inner] = jnp.zeros((lz, nx), jnp.float32)

    @pl.when(first_z)
    def _():
        zhalo[0] = jnp.zeros((ly, nx), jnp.float32)

    @pl.when(last_z)
    def _():
        zhalo[1] = jnp.zeros((ly, nx), jnp.float32)

    far_z[pl.ds(pl.multiple_of(mz * ly, 8), ly), :] = jnp.zeros((ly, nx), jnp.float32)
    corner_rows[...] = jnp.zeros_like(corner_rows)
    chold[mz] = jnp.zeros((1, 2 * nx), jnp.float32)

    pl.semaphore_wait(barrier, ny - 1 + nz - 1)

    def remote(src, dst, send, recv, target):
        return pltpu.make_async_remote_copy(
            src_ref=src, dst_ref=dst, send_sem=send, recv_sem=recv,
            device_id=target, device_id_type=MESH,
        )

    down_y = lax.rem(my + ny - 1, ny)
    up_y = lax.rem(my + 1, ny)
    down_z = lax.rem(mz + nz - 1, nz)
    up_z = lax.rem(mz + 1, nz)
    chunk = 512
    chunks = nx // chunk
    inside = (
        (jnp.logical_not(first_y), jnp.logical_not(last_y)),
        (jnp.logical_not(first_z), jnp.logical_not(last_z)),
    )
    ends = []
    for n in range(chunks):
        cols = pl.ds(n * chunk, chunk)
        mid = pl.ds(n * chunk + LANES, chunk)
        y_down = remote(
            heat.at[0, :, cols], field.at[ly + 1, :, mid],
            hs_send.at[0, n], hs_recv.at[0, n], {"gy": down_y},
        )
        y_up = remote(
            heat.at[ly - 1, :, cols], field.at[0, :, mid],
            hs_send.at[1, n], hs_recv.at[1, n], {"gy": up_y},
        )
        z_down = remote(
            zsend.at[0, :, cols], zhalo.at[1, :, cols],
            hs_send.at[2, n], hs_recv.at[2, n], {"gz": down_z},
        )
        z_up = remote(
            zsend.at[1, :, cols], zhalo.at[0, :, cols],
            hs_send.at[3, n], hs_recv.at[3, n], {"gz": up_z},
        )
        ends.append((
            (inside[0][0], y_down, y_up), (inside[0][1], y_up, y_down),
            (inside[1][0], z_down, z_up), (inside[1][1], z_up, z_down),
        ))
    for end in ends:
        for there, sent, _ in end[:2]:
            pl.when(there)(lambda sent=sent: sent.start())
    loads[0].wait()
    for y in range(ly):
        zsend[0, y : y + 1, :] = field[y + 1, 0:1, inner]
        zsend[1, y : y + 1, :] = field[y + 1, lz - 1 : lz, inner]
    for end in ends:
        for there, sent, _ in end[2:]:
            pl.when(there)(lambda sent=sent: sent.start())

    for load in loads[1:]:
        load.wait()
    weights = ey[...] * ez[...]
    w_own = split(weights[:, :rows])
    w_z = left_parts(weights[:, rows:off_y])
    w_y = left_parts(weights[:, off_y:off_c])
    w_c = left_parts(weights[:, off_c:total])
    toeplitz = tuple(
        jnp.concatenate([toep[2 * k, :, 0:XB], toep[2 * k + 1, :, 0:XB]], axis=0).astype(jnp.bfloat16)
        for k in range(2)
    )
    grow, fade = uw[0:1, 0:XB], uw[8:9, 0:XB]

    def column(owner):
        if owners % 2 or owners == 1:
            return pl.multiple_of(owner * cw, LANES)
        block = jnp.where(owner < half, 2 * owner, 2 * (owners - 1 - owner) + 1)
        return pl.multiple_of(block * cw, LANES)

    def owner_of(block):
        if owners % 2 or owners == 1:
            return block
        return block // 2 if block % 2 == 0 else owners - 1 - block // 2

    def to_owner(owner):
        return remote(
            yface.at[:, pl.ds(column(owner), cw)], held.at[my],
            a_send.at[owner], a_recv.at[my], {"gy": owner},
        )

    def from_peer(peer):
        return remote(
            yface.at[:, pl.ds(0, cw)], held.at[peer], a_send.at[0], a_recv.at[peer], {"gy": peer}
        )

    def owned(index, body):
        if owners == ny:
            body()
        else:
            pl.when(index < owners)(body)

    tile = lambda w: jnp.concatenate([w] * (chunk // LANES), axis=1)
    rise_z = tile(zw[0:8, 0:LANES])
    fall_z = tile(zw[8:16, 0:LANES])
    level = lax.broadcasted_iota(jnp.int32, (lz, chunk), 0)
    wide = chunk + 2 * LANES

    z_copies = []
    for x in range(0, nx, chunk):
        for there, _, received in ends[x // chunk]:
            pl.when(there)(lambda received=received: received.wait_recv())
        cols = pl.ds(x, chunk)
        mid = pl.ds(x + LANES, chunk)

        def layer(y, sums, x=x, cols=cols, mid=mid):
            window = field[y + 1, :, pl.ds(x, wide)]
            here = window[:, LANES : LANES + chunk]
            east = pltpu.roll(window, wide - 1, 1)[:, LANES : LANES + chunk]
            west = pltpu.roll(window, 1, 1)[:, LANES : LANES + chunk]
            south, north = field[y, :, mid], field[y + 2, :, mid]
            row = pl.ds(y, 1)
            above = jnp.where(level == lz - 1, zhalo[1, row, cols], pltpu.roll(here, lz - 1, 0))
            below = jnp.where(level == 0, zhalo[0, row, cols], pltpu.roll(here, 1, 0))
            spread = (east + west) + (north + south) + (above + below)
            moved = (
                vel[0, y, :, cols].astype(jnp.float32) * (east - west)
                + vel[1, y, :, cols].astype(jnp.float32) * (north - south)
                + vel[2, y, :, cols].astype(jnp.float32) * (above - below)
            )
            source = (1.0 - 6.0 * KAPPA) * here + KAPPA * spread - 0.5 * moved
            data[pl.ds(pl.multiple_of(y * lz, lz), lz), cols] = source
            zface[0, row, cols] = jnp.sum(source * rise_z, axis=0, keepdims=True)
            zface[1, row, cols] = jnp.sum(source * fall_z, axis=0, keepdims=True)
            rise_y = jnp.concatenate([coef[0, pl.ds(y, 1), 0:XB]] * (chunk // XB), axis=1)
            fall_y = jnp.concatenate([coef[1, pl.ds(y, 1), 0:XB]] * (chunk // XB), axis=1)
            return (sums[0] + rise_y * source, sums[1] + fall_y * source)

        zero = jnp.zeros((lz, chunk), jnp.float32)
        rising, falling = lax.fori_loop(0, ly, layer, (zero, zero), unroll=4)
        yface[0:lz, cols] = rising
        yface[lz : 2 * lz, cols] = falling
        for block in range(x // cw, (x + chunk) // cw):
            owner = owner_of(block)
            pl.when(my != owner)(lambda owner=owner: to_owner(owner).start())

        for d in range(1, nz):
            peer = lax.rem(mz + d, nz)
            side = (mz + d) // nz
            slot = far_z.at[pl.ds(pl.multiple_of(mz * ly, 8), ly), cols]
            n = x // chunk
            copy = remote(
                zface.at[side, :, cols], slot, z_send.at[peer, n], z_recv.at[mz, n], {"gz": peer}
            )
            copy.start()
            z_copies.append(copy)

    parts = [slice(a * XB, (a + 1) * XB) for a in range(blocks)]
    for part in parts:
        mixed[:, part] = dot3(w_own, split(data[:, part]))

    def to_peer(peer):
        return remote(
            back.at[peer], far_y.at[:, pl.ds(column(my), cw)],
            b_send.at[peer], b_recv.at[my], {"gy": peer},
        )

    def from_owner(owner):
        return remote(
            back.at[0], far_y.at[:, pl.ds(column(owner), cw)],
            b_send.at[0], b_recv.at[owner], {"gy": owner},
        )

    def gather_sums():
        held[my] = yface[:, pl.ds(column(my), cw)]
        for d in range(1, ny):
            from_peer(lax.rem(my + d, ny)).wait_recv()
        run = jnp.zeros((lz, cw), jnp.float32)
        for a in range(ny):
            back[a, 0:lz, :] = run
            run = run + held[a, 0:lz, :]
        run = jnp.zeros((lz, cw), jnp.float32)
        for a in reversed(range(ny)):
            back[a, lz : 2 * lz, :] = run
            run = run + held[a, lz : 2 * lz, :]
        for d in range(1, ny):
            to_peer(lax.rem(my + d, ny)).start()
        far_y[:, pl.ds(column(my), cw)] = back[my]

    owned(my, gather_sums)

    for d in range(1, nz):
        peer = lax.rem(mz + d, nz)
        for n in range(chunks):
            cols = pl.ds(n * chunk, chunk)
            slot = far_z.at[pl.ds(pl.multiple_of(peer * ly, 8), ly), cols]
            remote(
                zface.at[0, :, cols], slot, z_send.at[0, n], z_recv.at[peer, n], {"gz": peer}
            ).wait_recv()
    both = [mixed[:, part] + dot_left(w_z, far_z[:, part]) for part in parts]
    for part, piece in zip(parts, along_x(both, toeplitz, grow, fade)):
        acc[:, part] = piece

    for d in range(1, ny):
        owner = lax.rem(my + d, ny)
        owned(owner, lambda owner=owner: from_owner(owner).wait_recv())

    whole = lambda w: jnp.concatenate([w] * (nx // LANES), axis=1)
    for side in range(2):
        weight = whole(zw[8 * side : 8 * side + 8, 0:LANES])
        for k in range(2):
            far = far_y[k * lz : (k + 1) * lz, :]
            cface[side, :, k * nx : (k + 1) * nx] = jnp.sum(far * weight, axis=0, keepdims=True)
    c_copies = []
    for d in range(1, nz):
        peer = lax.rem(mz + d, nz)
        side = (mz + d) // nz
        copy = remote(cface.at[side], chold.at[mz], c_send.at[peer], c_recv.at[mz], {"gz": peer})
        copy.start()
        c_copies.append(copy)

    solved = along_x([far_y[:, part] for part in parts], toeplitz, grow, fade)
    for part, piece in zip(parts, solved):
        acc[:, part] += dot_left(w_y, piece)

    for d in range(1, nz):
        peer = lax.rem(mz + d, nz)
        remote(
            cface.at[0], chold.at[peer], c_send.at[0], c_recv.at[peer], {"gz": peer}
        ).wait_recv()
    for b in range(nz):
        for k in range(2):
            corner_rows[2 * b + k : 2 * b + k + 1, :] = chold[b, :, k * nx : (k + 1) * nx]
    solved = along_x([corner_rows[:, part] for part in parts], toeplitz, grow, fade)
    stores = []
    for a, (part, piece) in enumerate(zip(parts, solved)):
        acc[:, part] += dot_left(w_c, piece)
        place = pl.ds(a * XB, XB)
        stores.append(pltpu.make_async_copy(acc.at[:, place], out.at[:, place], out_sem.at[a]))
        stores[-1].start()

    for end in ends:
        for there, sent, _ in end:
            pl.when(there)(lambda sent=sent: sent.wait_send())
    for block in range(owners):
        owner = owner_of(block)
        pl.when(my != owner)(lambda owner=owner: to_owner(owner).wait_send())
    for copy in z_copies + c_copies:
        copy.wait_send()

    def sums_sent():
        for d in range(1, ny):
            to_peer(lax.rem(my + d, ny)).wait_send()

    owned(my, sums_sent)
    for store in stores:
        store.wait()


def on_device(ny, nz, heat, speed):
    ly, lz, nx = heat.shape
    rows, far_y, corner, total = sizes(ny, nz, ly, lz)
    owners = min(ny, nx // LANES)
    while (nx // LANES) % owners:
        owners -= 1
    cw = nx // owners
    coef, zw, ey, ez = tables(ny, nz, ly, lz)
    toep, uw = x_tables()
    wide = -(-total // XB) * XB
    table = np.zeros((ny + nz + 6 + -(-ny // 4), rows, wide), np.float32)
    table[:ny, :, :total] = ey
    table[ny : ny + nz, :, :total] = ez
    table[ny + nz : ny + nz + 4, :, :XB] = toep.astype(np.float32).reshape(4, rows, XB)
    table[ny + nz + 4, : 16 * nz, :LANES] = zw.reshape(16 * nz, LANES)
    table[ny + nz + 5, :16, :XB] = uw.reshape(16, XB)
    for a in range(ny):
        slab, row = ny + nz + 6 + a // 4, a % 4 * 32
        table[slab, row : row + 32] = coef.reshape(2, ny, ly)[:, a].reshape(32, 1)
    hbm = pl.BlockSpec(memory_space=pltpu.HBM)
    dma = pltpu.SemaphoreType.DMA
    f32 = jnp.float32
    out = pl.pallas_call(
        functools.partial(kernel, ny, nz, owners),
        out_shape=jax.ShapeDtypeStruct((rows, nx), f32),
        in_specs=[hbm] * 3,
        out_specs=hbm,
        scratch_shapes=[
            pltpu.VMEM((ly + 2, lz, nx + 2 * LANES), f32),
            pltpu.VMEM(speed.shape, speed.dtype),
            pltpu.VMEM((2, ly, nx), f32),
            pltpu.VMEM((2, ly, nx), f32),
            pltpu.VMEM((rows, nx), f32),
            pltpu.VMEM((nz * ly, nx), f32),
            pltpu.VMEM((2 * lz, nx), f32),
            pltpu.VMEM((total - corner, nx), f32),
            pltpu.VMEM((rows, nx), f32),
            pltpu.VMEM((rows, nx), f32),
            pltpu.VMEM((2 * lz, nx), f32),
            pltpu.VMEM((2, ly, nx), f32),
            pltpu.VMEM((ny, 2 * lz, cw), f32),
            pltpu.VMEM((ny, 2 * lz, cw), f32),
            pltpu.VMEM((2, 1, 2 * nx), f32),
            pltpu.VMEM((nz, 1, 2 * nx), f32),
            pltpu.VMEM((2, 16, wide), f32),
            pltpu.VMEM((16, wide), f32),
            pltpu.VMEM((rows, wide), f32),
            pltpu.VMEM((rows, wide), f32),
            pltpu.VMEM((4, rows, wide), f32),
            pltpu.VMEM((16, wide), f32),
            dma((9,)), dma((nx // XB,)), dma((4, nx // 512)), dma((4, nx // 512)),
            dma((ny,)), dma((ny,)), dma((ny,)), dma((ny,)),
            dma((nz, nx // 512)), dma((nz, nx // 512)), dma((nz,)), dma((nz,)),
        ],
        compiler_params=pltpu.CompilerParams(collective_id=0, has_side_effects=True, vmem_limit_bytes=53336 * 1024),
    )(heat, speed, jnp.asarray(table))
    return out.reshape(ly, lz, nx)


def solution(mesh):
    in_specs = (P("gy", "gz", None), P(None, "gy", "gz", None))
    return jax.shard_map(
        functools.partial(on_device, mesh.shape["gy"], mesh.shape["gz"]),
        mesh=mesh, in_specs=in_specs, out_specs=P("gy", "gz", None), check_vma=False,
    )
```
